32 devices in a mesh: ctx: 32 (over z, y, x, core), tp: 1.
Axes of the slice: x: 2, y: 2, z: 4, core: 2. Of those that a mesh axis runs over, the one named last changes fastest.
Arguments:
- streams: bfloat16 [3, 4096, 8192], P(None, 'ctx', 'tp'), may hold values from -6 to 6
- short_filter: float32 [3, 7, 512], P(None, None, 'tp'), may hold values from -2.5 to 2.5
- residues: float32 [16, 512], P(None, 'tp'), may hold values from -0.125 to 0.125
- rates: float32 [16, 512], P(None, 'tp'), may hold values from 2.4414062e-06 to 0.04
- skip: float32 [8192], P('tp'), may hold values from 0.5 to 1.5
- out_weight: bfloat16 [4096, 8192], P('ctx', 'tp'), may hold values from -0.0625 to 0.0625
- out_cotangent: bfloat16 [4096, 4096], P('ctx', 'tp'), may hold values from -12 to 12
Outputs:
- output: bfloat16 [4096, 4096], P('ctx', 'tp')
- grad_streams: bfloat16 [3, 4096, 8192], P(None, 'ctx', 'tp')
- grad_short: float32 [3, 7, 512], P(None, None, 'tp')
- grad_skip: float32 [8192], P('tp')
- grad_weight: float32 [4096, 8192], P('ctx', 'tp')
The draws below stay inside these ranges and needn't reach their ends.
All inputs are finite; a program needn't handle non-finite values.
Results may differ from the reference program's by a relative error of at most 0.034.
Values may be sent and summed in bfloat16 or wider, within the bound.
No kernel may reach another device: no remote copies, remote signals or barrier semaphores. Data moves between devices by JAX's collectives and lax.ppermute only.
A program may use at most 320 MiB of HBM per device.

```python
import math
import jax
import jax.numpy as jnp
from jax import lax

D = 8192
DOUT = 4096
MODES = 16
TAPS = 7
TOK_DEV = 128
GROUPS = 512
SEQ = 4096
N_TP = 1


def with_spikes(entries, rng, source, target, shards_of, factor):
    def block_of(position):
        return (jnp.arange(entries.shape[position]) // (entries.shape[position] // shards_of)).reshape((-1,) + (1,) * (entries.ndim - 1 - position))

    near = jax.random.permutation(rng, shards_of)[block_of(target)]
    other_side = (block_of(target) + shards_of // 2) % shards_of
    return jnp.where((block_of(source) == near) | (block_of(source) == other_side), factor * entries, entries)


def levels(key, dims, shards, least, top_value):
    def one(axis_at, parts):
        steps = jax.random.uniform(jax.random.fold_in(jax.random.fold_in(key, 6), axis_at), (parts,), jnp.float32, least / len(shards), top_value / len(shards))
        return jnp.repeat(jnp.exp(steps), dims[axis_at] // parts).reshape((-1,) + (1,) * (len(dims) - axis_at - 1))

    level = one(*shards[0])
    for cut in shards[1:]:
        level = level * one(*cut)
    return level


def normal_values(rng, extent, deviation, bound, cuts=(), kind=jnp.bfloat16):
    array = deviation * jax.random.normal(rng, extent, jnp.float32)
    if cuts:
        array = array * levels(rng, extent, cuts, -0.22, 0.18)
    return jnp.clip(array, -bound, bound).astype(kind)


def heavy_noise(stream_key, dims, spread, bound, cuts, heavy, held_as=jnp.bfloat16):
    drawn = spread * jax.random.normal(stream_key, dims, jnp.float32)
    if cuts:
        drawn = drawn * levels(stream_key, dims, cuts, -0.22, 0.18)
    return jnp.clip(with_spikes(drawn, jax.random.fold_in(stream_key, 3), *heavy), -bound, bound).astype(held_as)


def setup_inputs(seed: int = 0) -> dict:
    splits = jax.random.split(jax.random.key(seed), 8)
    streams = normal_values(splits[0], (3, SEQ, D), 1.0, 6.0, ((1, 32),))
    short_filter = normal_values(splits[1], (3, TAPS, GROUPS), 0.4, 2.5, (), jnp.float32)
    residues = normal_values(splits[2], (MODES, GROUPS), 0.02, 0.125, (), jnp.float32)
    rates = jnp.clip(jnp.exp(jax.random.uniform(splits[3], (MODES, GROUPS), jnp.float32, math.log(2.441406195430318e-06), math.log(0.04))), 2.441406195430318e-06, 0.04)
    skip = jnp.clip(jax.random.uniform(splits[4], (D,), jnp.float32, 0.5, 1.5), 0.5, 1.5)
    out_weight = normal_values(splits[5], (DOUT, D), D ** -0.5, 0.0625, ((0, 32),))
    out_cotangent = heavy_noise(splits[6], (SEQ, DOUT), 1.0, 12.0, ((0, 32),), (0, 1, 32, 2.75))
    return {"streams": streams, "short_filter": short_filter, "residues": residues, "rates": rates, "skip": skip, "out_weight": out_weight, "out_cotangent": out_cotangent}


highest = lax.Precision.HIGHEST


def causal_modal(source, residues, rates):
    total_rows, channels = source.shape
    groups = residues.shape[1]
    members = channels // groups
    length = math.gcd(32, total_rows)
    positions = jnp.arange(length, dtype=jnp.float32)
    profile = jnp.sum(residues[:, None, :] * jnp.exp(-rates[:, None, :] * positions[None, :, None]), axis=0)
    counter = jnp.arange(length, dtype=jnp.int32)
    offset = counter[:, None] - counter[None, :]
    toeplitz = jnp.where((offset >= 0)[:, :, None], jnp.take(profile, jnp.maximum(offset, 0).astype(jnp.int32), axis=0), jnp.float32(0.0))
    inflow = jnp.exp(-rates[None] * (length - 1.0 - positions)[:, None, None])
    carried = residues[None] * jnp.exp(-rates[None] * (positions + 1.0)[:, None, None])
    decay = jnp.exp(-rates * length)
    blocks = source.reshape(total_rows // length, length, groups, members)

    def advance(state, part):
        local = jnp.einsum("tsg,sgc->tgc", toeplitz, part, precision=highest)
        local = local + jnp.einsum("tmg,mgc->tgc", carried, state, precision=highest)
        state = decay[:, :, None] * state + jnp.einsum("smg,sgc->mgc", inflow, part, precision=highest)
        return state, local

    initial = jnp.zeros((residues.shape[0], groups, members), dtype=jnp.float32)
    _, pieces = lax.scan(advance, initial, blocks)
    return pieces.reshape(total_rows, channels)


def reference(streams, short_filter, residues, rates, skip, out_weight, out_cotangent):
    total_rows = streams.shape[1]
    channels = streams.shape[2]
    groups = residues.shape[1]
    members = channels // groups
    reach = short_filter.shape[1] - 1
    taps = jnp.repeat(short_filter, members, axis=2)
    padded = jnp.pad(streams, ((0, 0), (reach, 0), (0, 0)))
    smoothed = jnp.zeros(streams.shape, jnp.float32)
    for lag in range(reach + 1):
        smoothed = smoothed + taps[:, lag, None, :] * padded[:, reach - lag:reach - lag + total_rows, :].astype(jnp.float32)
    mixed = lax.optimization_barrier((smoothed[1] * smoothed[2]).astype(jnp.bfloat16)).astype(jnp.float32)
    field = causal_modal(mixed, residues, rates) + skip * mixed
    gated = (smoothed[0] * field).astype(jnp.bfloat16)
    block_channels = channels // N_TP
    output_sum = jnp.zeros((total_rows, out_weight.shape[0]), jnp.float32)
    for member in range(N_TP):
        first = member * block_channels
        term = jnp.dot(gated[:, first:first + block_channels], out_weight[:, first:first + block_channels].T, preferred_element_type=jnp.float32)
        output_sum = output_sum + lax.optimization_barrier(term.astype(jnp.bfloat16)).astype(jnp.float32)
    output = output_sum.astype(jnp.bfloat16)
    upstream = jnp.dot(out_cotangent, out_weight, preferred_element_type=jnp.float32)

    def accumulate(total, index):
        cot_rows = lax.dynamic_slice_in_dim(out_cotangent, (index * TOK_DEV).astype(jnp.int32), TOK_DEV, 0)
        gate_rows = lax.dynamic_slice_in_dim(gated, (index * TOK_DEV).astype(jnp.int32), TOK_DEV, 0)
        term = lax.dot_general(cot_rows, gate_rows, (((0,), (0,)), ((), ())), preferred_element_type=jnp.float32)
        return total + lax.optimization_barrier(term.astype(jnp.bfloat16)).astype(jnp.float32), None

    grad_weight, _ = lax.scan(accumulate, jnp.zeros(out_weight.shape, jnp.float32), jnp.arange(total_rows // TOK_DEV, dtype=jnp.int32))
    grad_field = upstream * smoothed[0]
    grad_skip = jnp.sum(grad_field * mixed, axis=0)
    grad_mixed = causal_modal(grad_field[::-1], residues, rates)[::-1] + skip * grad_field
    grad_smoothed = jnp.stack([upstream * field, grad_mixed * smoothed[2], grad_mixed * smoothed[1]])
    tap_rows = []
    for lag in range(reach + 1):
        product = grad_smoothed * padded[:, reach - lag:reach - lag + total_rows, :].astype(jnp.float32)
        tap_rows.append(jnp.sum(product.reshape(3, total_rows, groups, members), axis=(1, 3)))
    grad_short = jnp.stack(tap_rows, axis=1)
    padded_back = jnp.pad(grad_smoothed, ((0, 0), (0, reach), (0, 0)))
    grad_streams = jnp.zeros(streams.shape, jnp.float32)
    for lag in range(reach + 1):
        grad_streams = grad_streams + taps[:, lag, None, :] * padded_back[:, lag:lag + total_rows, :]
    return output, grad_streams.astype(jnp.bfloat16), grad_short, grad_skip, grad_weight
```

```python
import functools
import math

import jax
import jax.numpy as jnp
from jax import lax
from jax.experimental import pallas as pl
from jax.experimental.pallas import tpu as pltpu
from jax.sharding import Mesh, PartitionSpec as P

LANES = 128
EDGE = 8
STEP = 8
VMEM = 48 * 1024 * 1024


def at(token, rows):
    start = token * rows
    return pl.ds(start if isinstance(start, int) else pl.multiple_of(start, rows), rows)


def total_of(terms):
    while len(terms) > 1:
        terms = [
            terms[k] + terms[k + 1] if k + 1 < len(terms) else terms[k]
            for k in range(0, len(terms), 2)
        ]
    return terms[0]


def to_token_rows(ref, first, value, rows):
    count = value.shape[0]
    for j in range(rows):
        ref[pl.ds(first * rows + j, count, stride=rows), :] = value[
            :, j * LANES : (j + 1) * LANES
        ].astype(jnp.float32)


def smooth_kernel(
    rows, tok, x_ref, rim_ref, taps_ref, decay_ref, sm_ref, mixed_ref, xt_ref, end_ref, pad, state
):
    modes, lags = decay_ref.shape[0], taps_ref.shape[1]
    first = pl.program_id(0) == 0

    @pl.when(first)
    def _():
        for i in range(3):
            to_token_rows(pad.at[i], 0, rim_ref[i], rows)
        state[...] = jnp.zeros_like(state)

    @pl.when(jnp.logical_not(first))
    def _():
        for i in range(3):
            pad[i, pl.ds(0, EDGE * rows), :] = pad[i, pl.ds(tok * rows, EDGE * rows), :]

    for i in range(3):
        to_token_rows(pad.at[i], EDGE, x_ref[0, i], rows)
        xt_ref[i] = pad[i, pl.ds(EDGE * rows, tok * rows), :]

    def smooth(n, carry):
        base = n * STEP
        results = []
        for i in range(3):
            taps = [taps_ref[i, j] for j in range(lags)]
            window = [
                pad[i, at(base + EDGE - (lags - 1) + k, rows), :] for k in range(STEP + lags - 1)
            ]
            results.append(
                [
                    total_of([taps[j] * window[u + lags - 1 - j] for j in range(lags)])
                    for u in range(STEP)
                ]
            )
            for u in range(STEP):
                sm_ref[i, at(base + u, rows), :] = results[i][u]
        for u in range(STEP):
            mixed_ref[at(base + u, rows), :] = (
                (results[1][u] * results[2][u]).astype(jnp.bfloat16).astype(jnp.float32)
            )
        return carry

    lax.fori_loop(0, tok // STEP, smooth, 0)
    decay = [decay_ref[m] for m in range(modes)]

    def advance(n, held):
        held = list(held)
        for u in range(STEP):
            x = mixed_ref[at(n * STEP + u, rows), :]
            held = [decay[m] * held[m] + x for m in range(modes)]
        return tuple(held)

    held = lax.fori_loop(0, tok // STEP, advance, tuple(state[m] for m in range(modes)))
    for m in range(modes):
        state[m] = held[m]
        end_ref[m] = held[m]


def field_kernel(
    rows,
    tok,
    mixed_ref,
    sm_ref,
    before_ref,
    decay_ref,
    residue_ref,
    skip_ref,
    field_ref,
    gated_ref,
    staged,
    state,
):
    modes = decay_ref.shape[0]

    @pl.when(pl.program_id(0) == 0)
    def _():
        state[...] = before_ref[...]

    decay = [decay_ref[m] for m in range(modes)]
    residue = [residue_ref[m] for m in range(modes)]
    skip = skip_ref[...]

    def advance(n, held):
        held = list(held)
        for u in range(STEP):
            place = at(n * STEP + u, rows)
            x = mixed_ref[place, :]
            held = [decay[m] * held[m] + x for m in range(modes)]
            field = total_of([residue[m] * held[m] for m in range(modes)] + [skip * x])
            field_ref[place, :] = field
            staged[place, :] = sm_ref[0, place, :] * field
        return tuple(held)

    held = lax.fori_loop(0, tok // STEP, advance, tuple(state[m] for m in range(modes)))
    for m in range(modes):
        state[m] = held[m]
    for j in range(rows):
        gated_ref[:, j * LANES : (j + 1) * LANES] = staged[
            pl.ds(j, tok, stride=rows), :
        ].astype(jnp.bfloat16)


def cotangent_kernel(
    rows, tok, up_ref, sm_ref, mixed_ref, decay_ref, upt_ref, end_ref, gskip_ref, state, total
):
    modes = decay_ref.shape[0]

    @pl.when(pl.program_id(0) == 0)
    def _():
        state[...] = jnp.zeros_like(state)
        total[...] = jnp.zeros_like(total)

    to_token_rows(upt_ref, 0, up_ref[...], rows)
    decay = [decay_ref[m] for m in range(modes)]

    def retreat(n, carry):
        held, summed = list(carry[:-1]), carry[-1]
        for u in range(STEP):
            place = at(tok - 1 - (n * STEP + u), rows)
            grad = upt_ref[place, :] * sm_ref[0, place, :]
            summed = summed + grad * mixed_ref[place, :]
            held = [decay[m] * held[m] + grad for m in range(modes)]
        return tuple(held) + (summed,)

    carry = lax.fori_loop(
        0, tok // STEP, retreat, tuple(state[m] for m in range(modes)) + (total[...],)
    )
    for m in range(modes):
        state[m] = carry[m]
        end_ref[m] = carry[m]
    total[...] = carry[-1]
    gskip_ref[...] = carry[-1]


def back_kernel(
    rows,
    tok,
    upt_ref,
    sm_ref,
    field_ref,
    xt_ref,
    after_ref,
    decay_ref,
    residue_ref,
    skip_ref,
    taps_ref,
    out_ref,
    gtaps_ref,
    head_ref,
    tail_ref,
    pad,
    staged,
    state,
    total,
):
    modes, lags = decay_ref.shape[0], taps_ref.shape[1]
    first = pl.program_id(0) == 0

    @pl.when(first)
    def _():
        state[...] = after_ref[...]
        total[...] = jnp.zeros_like(total)
        for i in range(3):
            pad[i, pl.ds(tok * rows, EDGE * rows), :] = jnp.zeros((EDGE * rows, LANES), jnp.float32)

    @pl.when(jnp.logical_not(first))
    def _():
        for i in range(3):
            pad[i, pl.ds(tok * rows, EDGE * rows), :] = pad[i, pl.ds(0, EDGE * rows), :]

    decay = [decay_ref[m] for m in range(modes)]
    residue = [residue_ref[m] for m in range(modes)]
    skip = skip_ref[...]

    def retreat(n, held):
        held = list(held)
        for u in range(STEP):
            place = at(tok - 1 - (n * STEP + u), rows)
            up = upt_ref[place, :]
            grad = up * sm_ref[0, place, :]
            held = [decay[m] * held[m] + grad for m in range(modes)]
            mixed = total_of([residue[m] * held[m] for m in range(modes)] + [skip * grad])
            pad[0, place, :] = up * field_ref[place, :]
            pad[1, place, :] = mixed * sm_ref[2, place, :]
            pad[2, place, :] = mixed * sm_ref[1, place, :]
        return tuple(held)

    held = lax.fori_loop(0, tok // STEP, retreat, tuple(state[m] for m in range(modes)))
    for m in range(modes):
        state[m] = held[m]

    @pl.when(first)
    def _():
        for i in range(3):
            tail_ref[i] = pad[i, pl.ds((tok - EDGE) * rows, EDGE * rows), :]

    for i in range(3):
        head_ref[i] = pad[i, pl.ds(0, EDGE * rows), :]
        taps = [taps_ref[i, j] for j in range(lags)]

        def spread(n, sums, i=i, taps=taps):
            base = n * STEP
            sums = list(sums)
            window = [pad[i, at(base + k, rows), :] for k in range(STEP + lags - 1)]
            for u in range(STEP):
                x = xt_ref[i, at(base + u, rows), :]
                for j in range(lags):
                    sums[j] = sums[j] + x * window[u + j]
                staged[at(base + u, rows), :] = total_of(
                    [taps[j] * window[u + j] for j in range(lags)]
                )
            return tuple(sums)

        sums = lax.fori_loop(
            0, tok // STEP, spread, tuple(total[i, j] for j in range(lags))
        )
        for j in range(lags):
            total[i, j] = sums[j]
            gtaps_ref[i, j] = sums[j]
        for j in range(rows):
            out_ref[0, i, :, j * LANES : (j + 1) * LANES] = staged[
                pl.ds(j, tok, stride=rows), :
            ].astype(jnp.bfloat16)


def whole(shape):
    return pl.BlockSpec(shape, lambda n: (0,) * len(shape))


def call(kernel, name, blocks, ins, in_specs, outs, out_specs, scratch, ops):
    size = sum(math.prod(a.shape) * a.dtype.itemsize for a in list(ins) + list(outs))
    return pl.pallas_call(
        kernel,
        grid=(blocks,),
        in_specs=in_specs,
        out_specs=out_specs,
        out_shape=outs,
        scratch_shapes=scratch,
        compiler_params=pltpu.CompilerParams(vmem_limit_bytes=VMEM),
        cost_estimate=pl.CostEstimate(flops=ops, bytes_accessed=size, transcendentals=0),
        name=name,
    )(*ins)


def shards(streams, short_filter, residues, rates, skip, out_weight, out_cotangent):
    hi, lo = lax.axis_size("hi"), lax.axis_size("lo")
    plane, place = lax.axis_index("hi"), lax.axis_index("lo")
    tok, channels = streams.shape[1:]
    modes, groups = residues.shape
    members = channels // groups
    lags = short_filter.shape[1]
    wide, near = channels // lo, groups // lo
    rows = wide // LANES
    length = tok * lo
    f32 = jnp.float32
    shape = jax.ShapeDtypeStruct

    def mine(a):
        a = lax.dynamic_slice_in_dim(a, place * near, near, a.ndim - 1)
        return jnp.repeat(a, members, axis=-1).reshape(a.shape[:-1] + (rows, LANES))

    taps, residue, rate = mine(short_filter), mine(residues), mine(rates)
    decay = jnp.exp(-rate)
    plane_decay = jnp.exp(-rate * length)
    direct = lax.dynamic_slice_in_dim(skip, place * wide, wide, 0).reshape(rows, LANES)

    own = lax.all_to_all(out_weight.reshape(out_weight.shape[0], lo, wide), "lo", 1, 0)
    weights = lax.all_gather(own.reshape(-1, wide), "hi", axis=0, tiled=True)
    cotangent = lax.all_gather(out_cotangent, "tp", axis=1, tiled=True)
    cotangent = lax.all_gather(cotangent, "lo", axis=0, tiled=True)
    x = lax.all_to_all(streams.reshape(3, tok, lo, wide), "lo", 2, 0)

    forward = [(i, i + 1) for i in range(hi - 1)]
    backward = [(i + 1, i) for i in range(hi - 1)]
    rim = lax.ppermute(x[lo - 1, :, tok - EDGE :, :], "hi", forward).astype(f32)

    flat = tok * rows
    up_blocks = pl.BlockSpec((flat, LANES), lambda n: (n, 0))
    up_three = pl.BlockSpec((3, flat, LANES), lambda n: (0, n, 0))
    up_one = pl.BlockSpec((1, flat, LANES), lambda n: (0, n, 0))
    down_blocks = pl.BlockSpec((flat, LANES), lambda n: (lo - 1 - n, 0))
    down_three = pl.BlockSpec((3, flat, LANES), lambda n: (0, lo - 1 - n, 0))
    down_one = pl.BlockSpec((1, flat, LANES), lambda n: (0, lo - 1 - n, 0))
    taps_spec = whole((3, lags, rows, LANES))
    mode_spec = whole((modes, rows, LANES))
    skip_spec = whole((rows, LANES))
    edge_spec = whole((3, EDGE * rows, LANES))
    states = pltpu.VMEM((modes, rows, LANES), f32)
    padded = pltpu.VMEM((3, (tok + EDGE) * rows, LANES), f32)
    work = length * wide

    smoothed, mixed, xt, ending = call(
        functools.partial(smooth_kernel, rows, tok),
        "smooth",
        lo,
        (x, rim, taps, decay),
        [
            pl.BlockSpec((1, 3, tok, wide), lambda n: (n, 0, 0, 0)),
            whole((3, EDGE, wide)),
            taps_spec,
            mode_spec,
        ],
        [
            shape((3, length * rows, LANES), f32),
            shape((length * rows, LANES), f32),
            shape((3, length * rows, LANES), f32),
            shape((modes, rows, LANES), f32),
        ],
        [up_three, up_blocks, up_three, mode_spec],
        [padded, states],
        work * (6 * lags + 2 * modes),
    )

    def entering(end, later):
        gathered = lax.all_gather(end, "hi")
        held = jnp.zeros_like(end)
        for hop in reversed(range(hi)) if later else range(hi):
            used = hop > plane if later else hop < plane
            held = jnp.where(used, plane_decay * held + gathered[hop], held)
        return held

    before = entering(ending, False)
    field, gated = call(
        functools.partial(field_kernel, rows, tok),
        "field",
        lo,
        (mixed, smoothed, before, decay, residue, direct),
        [up_blocks, up_one, mode_spec, mode_spec, mode_spec, skip_spec],
        [shape((length * rows, LANES), f32), shape((length, wide), jnp.bfloat16)],
        [up_blocks, pl.BlockSpec((tok, wide), lambda n: (n, 0))],
        [pltpu.VMEM((flat, LANES), f32), states],
        work * 4 * modes,
    )

    partial_grad = lax.dot_general(
        cotangent, gated, (((0,), (0,)), ((), ())), preferred_element_type=f32
    ).astype(jnp.bfloat16)
    reduced = lax.psum_scatter(partial_grad, "hi", scatter_dimension=0, tiled=True)
    grad_weight = lax.all_to_all(reduced.reshape(lo, -1, wide), "lo", 0, 1)
    grad_weight = grad_weight.reshape(-1, channels).astype(f32)

    upstream = jnp.dot(cotangent, weights, preferred_element_type=f32)
    partial_out = lax.dot_general(
        gated, weights, (((1,), (1,)), ((), ())), preferred_element_type=f32
    ).astype(jnp.bfloat16)
    output = lax.psum_scatter(partial_out, "lo", scatter_dimension=0, tiled=True)
    output = lax.psum_scatter(output, "tp", scatter_dimension=1, tiled=True)

    upt, back_end, grad_skip = call(
        functools.partial(cotangent_kernel, rows, tok),
        "cotangent",
        lo,
        (upstream, smoothed, mixed, decay),
        [
            pl.BlockSpec((tok, wide), lambda n: (lo - 1 - n, 0)),
            down_one,
            down_blocks,
            mode_spec,
        ],
        [
            shape((length * rows, LANES), f32),
            shape((modes, rows, LANES), f32),
            shape((rows, LANES), f32),
        ],
        [down_blocks, mode_spec, skip_spec],
        [states, pltpu.VMEM((rows, LANES), f32)],
        work * (2 * modes + 3),
    )
    after = entering(back_end, True)
    grads, grad_taps, head, tail = call(
        functools.partial(back_kernel, rows, tok),
        "back",
        lo,
        (upt, smoothed, field, xt, after, decay, residue, direct, taps),
        [
            down_blocks,
            down_three,
            down_blocks,
            down_three,
            mode_spec,
            mode_spec,
            mode_spec,
            skip_spec,
            taps_spec,
        ],
        [
            shape((lo, 3, tok, wide), jnp.bfloat16),
            shape((3, lags, rows, LANES), f32),
            shape((3, EDGE * rows, LANES), f32),
            shape((3, EDGE * rows, LANES), f32),
        ],
        [
            pl.BlockSpec((1, 3, tok, wide), lambda n: (lo - 1 - n, 0, 0, 0)),
            taps_spec,
            edge_spec,
            edge_spec,
        ],
        [
            padded,
            pltpu.VMEM((flat, LANES), f32),
            states,
            pltpu.VMEM((3, lags, rows, LANES), f32),
        ],
        work * (4 * modes + 12 * lags),
    )

    beyond = lax.ppermute(head, "hi", backward).reshape(3, EDGE, rows, LANES)
    tail = tail.reshape(3, EDGE, rows, LANES)
    joined = jnp.concatenate([tail, beyond], axis=1)
    extra = jnp.concatenate([jnp.zeros_like(tail), beyond], axis=1)
    last = xt[:, -EDGE * rows :, :].reshape(3, EDGE, rows, LANES)
    ends = sum(taps[:, j, None] * joined[:, j : j + EDGE] for j in range(lags))
    grads = lax.dynamic_update_slice(
        grads,
        ends.reshape(1, 3, EDGE, wide).astype(jnp.bfloat16),
        (lo - 1, 0, tok - EDGE, 0),
    )
    grad_taps = grad_taps + jnp.stack(
        [jnp.sum(last * extra[:, j : j + EDGE], axis=1) for j in range(lags)], axis=1
    )
    grad_streams = lax.all_to_all(grads, "lo", 0, 2).reshape(3, tok, channels)

    grad_taps = jnp.sum(grad_taps.reshape(3 * lags * near, members), axis=1)
    small = jnp.concatenate([grad_skip.reshape(-1), grad_taps])
    small = jnp.sum(lax.all_gather(small, ("hi", "lo")).reshape(hi, lo, -1), axis=0)
    grad_skip = small[:, :wide].reshape(channels)
    grad_short = jnp.moveaxis(small[:, wide:].reshape(lo, 3, lags, near), 0, 2)
    return output, grad_streams, grad_short.reshape(3, lags, groups), grad_skip, grad_weight


def solution(mesh):
    count, parts = mesh.shape["ctx"], mesh.shape["tp"]
    lo = math.gcd(count, 8)
    cut = Mesh(mesh.devices.reshape(count // lo, lo, parts), ("hi", "lo", "tp"))
    ctx = ("hi", "lo")
    return jax.shard_map(
        shards,
        mesh=cut,
        in_specs=(
            P(None, ctx, "tp"),
            P(None, None, "tp"),
            P(None, "tp"),
            P(None, "tp"),
            P("tp"),
            P(ctx, "tp"),
            P(ctx, "tp"),
        ),
        out_specs=(
            P(ctx, "tp"),
            P(None, ctx, "tp"),
            P(None, None, "tp"),
            P("tp"),
            P(ctx, "tp"),
        ),
        check_vma=False,
    )
```

```python
import functools
import math

import jax
import jax.numpy as jnp
from jax import lax
from jax.experimental import pallas as pl
from jax.experimental.pallas import tpu as pltpu
from jax.sharding import Mesh, PartitionSpec as P

LANES = 128
EDGE = 8
STEP = 8
VMEM = 48 * 1024 * 1024


def at(token, rows):
    start = token * rows
    return pl.ds(start if isinstance(start, int) else pl.multiple_of(start, rows), rows)


def total_of(terms):
    while len(terms) > 1:
        terms = [
            terms[k] + terms[k + 1] if k + 1 < len(terms) else terms[k]
            for k in range(0, len(terms), 2)
        ]
    return terms[0]


def to_token_rows(ref, first, value, rows):
    count = value.shape[0]
    for j in range(rows):
        ref[pl.ds(first * rows + j, count, stride=rows), :] = value[
            :, j * LANES : (j + 1) * LANES
        ].astype(jnp.float32)


def fill(pad, parts, rims, rows, tok):
    first = pl.program_id(0) == 0

    @pl.when(first)
    def _():
        for i in range(pad.shape[0]):
            to_token_rows(pad.at[i], 0, rims[i], rows)

    @pl.when(jnp.logical_not(first))
    def _():
        for i in range(pad.shape[0]):
            pad[i, pl.ds(0, EDGE * rows), :] = pad[i, pl.ds(tok * rows, EDGE * rows), :]

    for i in range(pad.shape[0]):
        to_token_rows(pad.at[i], EDGE, parts[i], rows)


def rim_rows(rim_ref):
    rims = rim_ref[0].astype(jnp.float32)
    return [rims[i * EDGE : (i + 1) * EDGE] for i in range(3)]


def convolved(pad, i, taps, base, rows):
    lags = len(taps)
    window = [pad[i, at(base + EDGE - (lags - 1) + k, rows), :] for k in range(STEP + lags - 1)]
    return [
        total_of([taps[j] * window[u + lags - 1 - j] for j in range(lags)]) for u in range(STEP)
    ]


def smooth_kernel(
    rows,
    tok,
    x_ref,
    rim_ref,
    taps_ref,
    decay_ref,
    hold_ref,
    sm_ref,
    mixed_ref,
    xt_ref,
    end_ref,
    room_ref,
    pad,
    state,
):
    modes, lags = decay_ref.shape[0], taps_ref.shape[1]

    @pl.when(pl.program_id(0) == 0)
    def _():
        state[...] = jnp.zeros_like(state)

    parts = [x_ref[0, pl.ds(i * tok, tok), :] for i in range(2)]
    fill(pad, parts, rim_rows(rim_ref)[1:], rows, tok)
    for i in range(2):
        xt_ref[i] = pad[i, pl.ds(EDGE * rows, tok * rows), :]

    def smooth(n, carry):
        base = n * STEP
        results = []
        for i in range(2):
            taps = [taps_ref[i + 1, j] for j in range(lags)]
            results.append(convolved(pad, i, taps, base, rows))
            for u in range(STEP):
                sm_ref[i, at(base + u, rows), :] = results[i][u]
        for u in range(STEP):
            mixed_ref[at(base + u, rows), :] = (
                (results[0][u] * results[1][u]).astype(jnp.bfloat16).astype(jnp.float32)
            )
        return carry

    lax.fori_loop(0, tok // STEP, smooth, 0)
    decay = [decay_ref[m] for m in range(modes)]

    def advance(n, held):
        held = list(held)
        for u in range(STEP):
            x = mixed_ref[at(n * STEP + u, rows), :]
            held = [decay[m] * held[m] + x for m in range(modes)]
        return tuple(held)

    held = lax.fori_loop(0, tok // STEP, advance, tuple(state[m] for m in range(modes)))
    for m in range(modes):
        state[m] = held[m]
        end_ref[m] = held[m]


def field_kernel(
    rows,
    tok,
    x_ref,
    rim_ref,
    taps_ref,
    mixed_ref,
    before_ref,
    decay_ref,
    residue_ref,
    skip_ref,
    sm_ref,
    xt_ref,
    field_ref,
    gated_ref,
    pad,
    staged,
    state,
):
    modes, lags = decay_ref.shape[0], taps_ref.shape[1]

    @pl.when(pl.program_id(0) == 0)
    def _():
        state[...] = before_ref[...]

    fill(pad, [x_ref[0, 0]], rim_rows(rim_ref), rows, tok)
    xt_ref[...] = pad[0, pl.ds(EDGE * rows, tok * rows), :]
    taps = [taps_ref[0, j] for j in range(lags)]

    def smooth(n, carry):
        results = convolved(pad, 0, taps, n * STEP, rows)
        for u in range(STEP):
            sm_ref[at(n * STEP + u, rows), :] = results[u]
        return carry

    lax.fori_loop(0, tok // STEP, smooth, 0)
    decay = [decay_ref[m] for m in range(modes)]
    residue = [residue_ref[m] for m in range(modes)]
    skip = skip_ref[...]

    def advance(n, held):
        held = list(held)
        for u in range(STEP):
            place = at(n * STEP + u, rows)
            x = mixed_ref[place, :]
            held = [decay[m] * held[m] + x for m in range(modes)]
            field = total_of([residue[m] * held[m] for m in range(modes)] + [skip * x])
            field_ref[place, :] = field
            staged[place, :] = sm_ref[place, :] * field
        return tuple(held)

    held = lax.fori_loop(0, tok // STEP, advance, tuple(state[m] for m in range(modes)))
    for m in range(modes):
        state[m] = held[m]
    for j in range(rows):
        gated_ref[:, j * LANES : (j + 1) * LANES] = staged[
            pl.ds(j, tok, stride=rows), :
        ].astype(jnp.bfloat16)


def clear_or_shift(pad, rows, tok):
    first = pl.program_id(0) == 0

    @pl.when(first)
    def _():
        for i in range(pad.shape[0]):
            pad[i, pl.ds(tok * rows, EDGE * rows), :] = jnp.zeros((EDGE * rows, LANES), jnp.float32)

    @pl.when(jnp.logical_not(first))
    def _():
        for i in range(pad.shape[0]):
            pad[i, pl.ds(tok * rows, EDGE * rows), :] = pad[i, pl.ds(0, EDGE * rows), :]


def spread_back(
    rows, tok, i, pad, xt_at, taps, total, out_ref, gtaps_ref, staged
):
    lags = len(taps)

    def spread(n, sums):
        base = n * STEP
        sums = list(sums)
        window = [pad[i, at(base + k, rows), :] for k in range(STEP + lags - 1)]
        for u in range(STEP):
            x = xt_at(at(base + u, rows))
            for j in range(lags):
                sums[j] = sums[j] + x * window[u + j]
            staged[at(base + u, rows), :] = total_of(
                [taps[j] * window[u + j] for j in range(lags)]
            )
        return tuple(sums)

    sums = lax.fori_loop(0, tok // STEP, spread, tuple(total[i, j] for j in range(lags)))
    for j in range(lags):
        total[i, j] = sums[j]
        gtaps_ref[i, j] = sums[j]
    for j in range(rows):
        out_ref[0, i, :, j * LANES : (j + 1) * LANES] = staged[
            pl.ds(j, tok, stride=rows), :
        ].astype(jnp.bfloat16)


def cotangent_kernel(
    rows,
    tok,
    up_ref,
    gated_ref,
    sm_ref,
    mixed_ref,
    field_ref,
    xt_ref,
    taps_ref,
    decay_ref,
    grad_ref,
    mid_ref,
    end_ref,
    gskip_ref,
    out_ref,
    gtaps_ref,
    head_ref,
    tail_ref,
    kept_ref,
    pad,
    staged,
    state,
    summed,
    total,
):
    modes, lags = decay_ref.shape[0], taps_ref.shape[1]

    @pl.when(pl.program_id(0) == 0)
    def _():
        state[...] = jnp.zeros_like(state)
        summed[...] = jnp.zeros_like(summed)
        total[...] = jnp.zeros_like(total)

    kept_ref[...] = gated_ref[...]
    clear_or_shift(pad, rows, tok)
    to_token_rows(staged, 0, up_ref[...], rows)
    decay = [decay_ref[m] for m in range(modes)]

    def retreat(n, carry):
        held, added = list(carry[:-1]), carry[-1]
        for u in range(STEP):
            place = at(tok - 1 - (n * STEP + u), rows)
            up = staged[place, :]
            grad = up * sm_ref[place, :]
            grad_ref[place, :] = grad
            pad[0, place, :] = up * field_ref[place, :]
            added = added + grad * mixed_ref[place, :]
            held = [decay[m] * held[m] + grad for m in range(modes)]
        return tuple(held) + (added,)

    last = tok // STEP - 1
    carry = lax.fori_loop(
        0, last, retreat, tuple(state[m] for m in range(modes)) + (summed[...],)
    )
    for m in range(modes):
        mid_ref[m] = carry[m]
    carry = retreat(last, carry)
    for m in range(modes):
        state[m] = carry[m]
        end_ref[m] = carry[m]
    summed[...] = carry[-1]
    gskip_ref[...] = carry[-1]
    spread_back(
        rows,
        tok,
        0,
        pad,
        lambda place: xt_ref[place, :],
        [taps_ref[0, j] for j in range(lags)],
        total,
        out_ref,
        gtaps_ref,
        staged,
    )

    @pl.when(pl.program_id(0) == 0)
    def _():
        tail_ref[...] = pad[0, pl.ds((tok - EDGE) * rows, EDGE * rows), :]

    head_ref[...] = pad[0, pl.ds(0, EDGE * rows), :]


def back_kernel(
    rows,
    tok,
    grad_ref,
    sm_ref,
    xt_ref,
    after_ref,
    ahead_ref,
    decay_ref,
    residue_ref,
    skip_ref,
    taps_ref,
    out_ref,
    gtaps_ref,
    pad,
    staged,
    state,
    total,
):
    modes, lags = decay_ref.shape[0], taps_ref.shape[1]
    decay = [decay_ref[m] for m in range(modes)]
    residue = [residue_ref[m] for m in range(modes)]
    skip = skip_ref[...]

    @pl.when(pl.program_id(0) == 0)
    def _():
        total[...] = jnp.zeros_like(total)
        held = [after_ref[m] for m in range(modes)]
        for u in reversed(range(EDGE)):
            grad, one, two = [ahead_ref[at(k * EDGE + u, rows), :] for k in range(3)]
            held = [decay[m] * held[m] + grad for m in range(modes)]
            mixed = total_of([residue[m] * held[m] for m in range(modes)] + [skip * grad])
            pad[0, at(tok + u, rows), :] = mixed * two
            pad[1, at(tok + u, rows), :] = mixed * one
        for m in range(modes):
            state[m] = held[m]

    @pl.when(pl.program_id(0) != 0)
    def _():
        for i in range(2):
            pad[i, pl.ds(tok * rows, EDGE * rows), :] = pad[i, pl.ds(0, EDGE * rows), :]


    def retreat(n, held):
        held = list(held)
        for u in range(STEP):
            place = at(tok - 1 - (n * STEP + u), rows)
            grad = grad_ref[place, :]
            held = [decay[m] * held[m] + grad for m in range(modes)]
            mixed = total_of([residue[m] * held[m] for m in range(modes)] + [skip * grad])
            pad[0, place, :] = mixed * sm_ref[1, place, :]
            pad[1, place, :] = mixed * sm_ref[0, place, :]
        return tuple(held)

    held = lax.fori_loop(0, tok // STEP, retreat, tuple(state[m] for m in range(modes)))
    for m in range(modes):
        state[m] = held[m]
    for i in range(2):
        spread_back(
            rows,
            tok,
            i,
            pad,
            lambda place, i=i: xt_ref[i, place, :],
            [taps_ref[i + 1, j] for j in range(lags)],
            total,
            out_ref,
            gtaps_ref,
            staged,
        )


def whole(shape):
    return pl.BlockSpec(shape, lambda n: (0,) * len(shape))


def call(kernel, name, blocks, ins, in_specs, outs, out_specs, scratch, ops, aliases={}):
    return pl.pallas_call(
        kernel,
        grid=(blocks,),
        in_specs=in_specs,
        out_specs=out_specs,
        out_shape=outs,
        scratch_shapes=scratch,
        input_output_aliases=aliases,
        compiler_params=pltpu.CompilerParams(vmem_limit_bytes=VMEM),
        cost_estimate=pl.CostEstimate(flops=ops, bytes_accessed=0, transcendentals=0),
        name=name,
    )(*ins)


def tie_kernel(*refs):
    pass


def tie(values, after):
    values, after = tuple(values), tuple(after)
    held = pl.BlockSpec(memory_space=pl.ANY)
    return pl.pallas_call(
        tie_kernel,
        in_specs=[held] * (len(values) + len(after)),
        out_specs=[held] * len(values),
        out_shape=[jax.ShapeDtypeStruct(a.shape, a.dtype) for a in values],
        input_output_aliases={i: i for i in range(len(values))},
        compiler_params=pltpu.CompilerParams(vmem_limit_bytes=VMEM),
        name="tie",
    )(*values, *after)


def split_kernel(in_ref, out_ref):
    out_ref[0] = in_ref[...].astype(out_ref.dtype)


def split_channels(a, lo, first, count):
    tok, wide = a.shape[1], a.shape[2] // lo
    return call(
        split_kernel,
        "split",
        lo * count,
        (a,),
        [pl.BlockSpec((1, tok, wide), lambda n: (first + n // lo, 0, n % lo))],
        jax.ShapeDtypeStruct((lo, count, tok, wide), a.dtype),
        pl.BlockSpec((1, 1, tok, wide), lambda n: (n % lo, n // lo, 0, 0)),
        [],
        0,
    )


def pack_kernel(tok, x_ref, rim_ref, out_ref, first_ref):
    first_ref[0, 0] = x_ref[0]
    out_ref[0, pl.ds(0, tok), :] = x_ref[1]
    out_ref[0, pl.ds(tok, tok), :] = x_ref[2]
    rims = [rim_ref[i].astype(jnp.float32) for i in range(3)]
    rims.append(jnp.zeros_like(rims[0]))
    out_ref[0, pl.ds(2 * tok, 4 * EDGE), :] = jnp.concatenate(rims).astype(out_ref.dtype)


def pack(streams, rim, lo):
    tok, wide = streams.shape[1], streams.shape[2] // lo
    held = 2 * tok + 4 * EDGE
    return call(
        functools.partial(pack_kernel, tok),
        "pack",
        lo,
        (streams, rim),
        [
            pl.BlockSpec((3, tok, wide), lambda n: (0, 0, n)),
            pl.BlockSpec((3, EDGE, wide), lambda n: (0, 0, n)),
        ],
        [
            jax.ShapeDtypeStruct((lo, held, wide), streams.dtype),
            jax.ShapeDtypeStruct((lo, 1, tok, wide), streams.dtype),
        ],
        [
            pl.BlockSpec((1, held, wide), lambda n: (n, 0, 0)),
            pl.BlockSpec((1, 1, tok, wide), lambda n: (n, 0, 0, 0)),
        ],
        [],
        0,
    )


def join_kernel(*refs):
    out_ref, first = refs[-1], 0
    for ref in refs[:-1]:
        out_ref[pl.ds(first, ref.shape[1])] = ref[0].astype(out_ref.dtype)
        first += ref.shape[1]


def join_channels(pieces, dtype, tok):
    lo, _, _, wide = pieces[0].shape
    total = sum(piece.shape[1] for piece in pieces)
    return call(
        join_kernel,
        "join",
        lo,
        pieces,
        [
            pl.BlockSpec((1, piece.shape[1], tok, wide), lambda n: (n, 0, 0, 0))
            for piece in pieces
        ],
        jax.ShapeDtypeStruct((total, tok, lo * wide), dtype),
        pl.BlockSpec((total, tok, wide), lambda n: (0, 0, n)),
        [],
        0,
    )


class Planes:
    def __init__(self, block, hi, plane):
        self.block, self.hi, self.plane = block, hi, plane
        self.rows, self.done, self.placed = block.shape[0], 0, 0
        self.right, self.left = block, block
        self.arrived = []
        self.result = None

    def step(self):
        self.done += 1
        k, hi = self.done, self.hi
        self.right = lax.ppermute(self.right, "hi", [(z, z + 1) for z in range(k - 1, hi - 1)])
        self.left = lax.ppermute(self.left, "hi", [(z + 1, z) for z in range(hi - k)])
        self.arrived.append((self.right, self.left))

    def put(self, piece, there):
        valid = jnp.logical_and(there >= 0, there < self.hi)
        self.result = lax.dynamic_update_slice_in_dim(
            self.result,
            jnp.where(valid, piece, self.block),
            jnp.where(valid, there, self.plane) * self.rows,
            0,
        )

    def place(self):
        if not self.placed:
            self.put(self.block, self.plane)
        if self.done:
            self.arrived[-1] = (self.right, self.left)
        while self.placed < self.done:
            self.placed += 1
            k, (right, left) = self.placed, self.arrived[self.placed - 1]
            if 2 * k < self.hi:
                self.put(right, self.plane - k)
                self.put(left, self.plane + k)
            else:
                below = self.plane >= k
                self.put(
                    jnp.where(below, right, left),
                    jnp.where(below, self.plane - k, self.plane + k),
                )


class Sums:
    def __init__(self, partial, hi, plane):
        self.partial, self.hi, self.plane = partial, hi, plane
        self.rows, self.done = partial.shape[0] // hi, 0
        self.right, self.left = None, None

    def part(self, d):
        first = jnp.clip(d, 0, self.hi - 1) * self.rows
        return lax.dynamic_slice_in_dim(self.partial, first, self.rows, 0).astype(jnp.float32)

    def step(self):
        self.done += 1
        s, hi, dtype = self.done, self.hi, self.partial.dtype
        self.to_right = add(self.part(hi - s + self.plane), self.right).astype(dtype)
        self.to_left = add(self.part(s - hi + self.plane), self.left).astype(dtype)
        self.right = lax.ppermute(self.to_right, "hi", [(z, z + 1) for z in range(s)])
        self.left = lax.ppermute(
            self.to_left, "hi", [(hi - 1 - z, hi - 2 - z) for z in range(s)]
        )

    def finish(self):
        return add(add(self.part(self.plane), self.right), self.left)


def add(mine, arrived):
    return mine if arrived is None else mine + arrived.astype(jnp.float32)


def shards(streams, short_filter, residues, rates, skip, out_weight, out_cotangent):
    hi, lo = lax.axis_size("hi"), lax.axis_size("lo")
    plane, place = lax.axis_index("hi"), lax.axis_index("lo")
    tok, channels = streams.shape[1:]
    modes, groups = residues.shape
    members = channels // groups
    lags = short_filter.shape[1]
    wide, near = channels // lo, groups // lo
    rows = wide // LANES
    length = tok * lo
    f32 = jnp.float32
    shape = jax.ShapeDtypeStruct

    def mine(a):
        a = lax.dynamic_slice_in_dim(a, place * near, near, a.ndim - 1)
        return jnp.repeat(a, members, axis=-1).reshape(a.shape[:-1] + (rows, LANES))

    taps, residue, rate = mine(short_filter), mine(residues), mine(rates)
    decay = jnp.exp(-rate)
    plane_decay = jnp.exp(-rate * length)
    direct = lax.dynamic_slice_in_dim(skip, place * wide, wide, 0).reshape(rows, LANES)

    ends = [(z * lo - 1, z * lo) for z in range(1, hi)]
    rim = lax.ppermute(streams[:, tok - EDGE :, :], ("hi", "lo"), ends)
    own = lax.all_to_all(split_channels(out_weight[None], lo, 0, 1), "lo", 0, 0, tiled=True)
    own = own.reshape(-1, wide)
    packed12, packed0 = tie(pack(streams, rim, lo), (own,))
    x12 = lax.all_to_all(packed12, "lo", 0, 0, tiled=True)
    (packed0,) = tie((packed0,), (x12,))
    x0 = lax.all_to_all(packed0, "lo", 0, 0, tiled=True)
    (cotangent,) = tie((out_cotangent,), (x12,))
    cotangent = lax.all_gather(cotangent, "tp", axis=1, tiled=True)
    cotangent = lax.all_gather(cotangent, "lo", axis=0, tiled=True)

    flat = tok * rows
    tokens = length * rows
    up_one = pl.BlockSpec((flat, LANES), lambda n: (n, 0))
    up_two = pl.BlockSpec((2, flat, LANES), lambda n: (0, n, 0))
    up_wide = pl.BlockSpec((tok, wide), lambda n: (n, 0))
    down_one = pl.BlockSpec((flat, LANES), lambda n: (lo - 1 - n, 0))
    down_two = pl.BlockSpec((2, flat, LANES), lambda n: (0, lo - 1 - n, 0))
    down_wide = pl.BlockSpec((tok, wide), lambda n: (lo - 1 - n, 0))
    taps_spec = whole((3, lags, rows, LANES))
    mode_spec = whole((modes, rows, LANES))
    skip_spec = whole((rows, LANES))
    held_spec = pl.BlockSpec(memory_space=pl.ANY)
    states = pltpu.VMEM((modes, rows, LANES), f32)
    staged = pltpu.VMEM((flat, LANES), f32)
    work = length * wide

    def padded(count):
        return pltpu.VMEM((count, (tok + EDGE) * rows, LANES), f32)

    rim_spec = pl.BlockSpec((1, 4 * EDGE, wide), lambda n: (0, 2 * tok // (4 * EDGE), 0))

    def grads_spec(count):
        return pl.BlockSpec((1, count, tok, wide), lambda n: (lo - 1 - n, 0, 0, 0))

    mover = Planes(own, hi, plane)
    mover.step()

    sm12, mixed, xt12, ending, mover.result = call(
        functools.partial(smooth_kernel, rows, tok),
        "smooth",
        lo,
        (x12, x12, taps, decay, mover.right),
        [
            pl.BlockSpec((1, 2 * tok, wide), lambda n: (n, 0, 0)),
            rim_spec,
            taps_spec,
            mode_spec,
            held_spec,
        ],
        [
            shape((2, tokens, LANES), f32),
            shape((tokens, LANES), f32),
            shape((2, tokens, LANES), f32),
            shape((modes, rows, LANES), f32),
            shape((hi * own.shape[0], wide), own.dtype),
        ],
        [up_two, up_one, up_two, mode_spec, held_spec],
        [padded(2), states],
        0,
    )
    mover.step()

    def from_plane(a, distance):
        pairs = [(z + distance, z) for z in range(max(0, -distance), hi - max(0, distance))]
        return lax.ppermute(a, "hi", pairs)

    before = jnp.zeros_like(ending)
    for k in reversed(range(1, hi)):
        before = from_plane(ending, -k) + plane_decay * before
    mover.right, mover.left = tie((mover.right, mover.left), (before,))
    sm0, xt0, field, gated = call(
        functools.partial(field_kernel, rows, tok),
        "field",
        lo,
        (x0, x12, taps, mixed, before, decay, residue, direct),
        [
            pl.BlockSpec((1, 1, tok, wide), lambda n: (n, 0, 0, 0)),
            rim_spec,
            taps_spec,
            up_one,
            mode_spec,
            mode_spec,
            mode_spec,
            skip_spec,
        ],
        [
            shape((tokens, LANES), f32),
            shape((tokens, LANES), f32),
            shape((tokens, LANES), f32),
            shape((length, wide), jnp.bfloat16),
        ],
        [up_one, up_one, up_one, up_wide],
        [padded(1), staged, states],
        0,
    )
    mover.place()
    while mover.done < hi - 1:
        mover.step()

    partial_grad = lax.dot_general(
        cotangent, gated, (((0,), (0,)), ((), ())), preferred_element_type=f32
    ).astype(jnp.bfloat16)
    sums = Sums(partial_grad, hi, plane)
    sums.step()
    mover.right, mover.left = tie((mover.right, mover.left), (sums.to_right, sums.to_left))
    mover.place()
    weights = mover.result

    upstream = jnp.dot(cotangent, weights, preferred_element_type=f32)
    grad_field, back_mid, back_end, grad_skip, grads0, grad_taps0, head, tail, kept = call(
        functools.partial(cotangent_kernel, rows, tok),
        "cotangent",
        lo,
        (upstream, gated, sm0, mixed, field, xt0, taps, decay),
        [
            down_wide,
            down_wide,
            down_one,
            down_one,
            down_one,
            down_one,
            taps_spec,
            mode_spec,
        ],
        [
            shape((tokens, LANES), f32),
            shape((modes, rows, LANES), f32),
            shape((modes, rows, LANES), f32),
            shape((rows, LANES), f32),
            shape((lo, 1, tok, wide), jnp.bfloat16),
            shape((1, lags, rows, LANES), f32),
            shape((EDGE * rows, LANES), f32),
            shape((EDGE * rows, LANES), f32),
            shape(gated.shape, gated.dtype),
        ],
        [
            down_one,
            mode_spec,
            mode_spec,
            skip_spec,
            grads_spec(1),
            whole((1, lags, rows, LANES)),
            whole((EDGE * rows, LANES)),
            whole((EDGE * rows, LANES)),
            down_wide,
        ],
        [
            padded(1),
            staged,
            states,
            pltpu.VMEM((rows, LANES), f32),
            pltpu.VMEM((1, lags, rows, LANES), f32),
        ],
        0,
    )

    back_mid, back_end = tie((back_mid, back_end), (sums.right, sums.left))
    edge = EDGE * rows
    heads = [
        back_mid.reshape(-1, LANES),
        grad_field[:edge],
        sm12[0, :edge],
        sm12[1, :edge],
        head,
    ]
    ahead = from_plane(jnp.concatenate(heads), 1)
    beyond = jnp.zeros_like(back_end)
    for k in reversed(range(2, hi)):
        beyond = from_plane(back_end, k) + plane_decay * beyond
    after = ahead[: modes * rows].reshape(back_end.shape) + beyond * jnp.exp(
        -rate * (length - EDGE)
    )
    ahead = ahead[modes * rows :]

    edges = (EDGE, rows, LANES)
    beyond, tail = ahead[3 * edge :].reshape(edges), tail.reshape(edges)
    last = xt0[-edge:].reshape(edges)
    joined = jnp.concatenate([tail, beyond])
    extra = jnp.concatenate([jnp.zeros_like(tail), beyond])
    fixed = sum(taps[0, j] * joined[j : j + EDGE] for j in range(lags))
    grads0 = lax.dynamic_update_slice(
        grads0,
        fixed.reshape(1, 1, EDGE, wide).astype(grads0.dtype),
        (lo - 1, 0, tok - EDGE, 0),
    )
    grad_taps0 = grad_taps0[0] + jnp.stack(
        [jnp.sum(last * extra[j : j + EDGE], axis=0) for j in range(lags)]
    )
    grads0 = lax.all_to_all(grads0, "lo", 0, 0, tiled=True)

    sums.right, sums.left = tie((sums.right, sums.left), (after, ahead))
    sums.step()
    (kept,) = tie((kept,), (sums.to_right, sums.to_left))
    partial_out = lax.dot_general(
        kept, weights, (((1,), (1,)), ((), ())), preferred_element_type=f32
    ).astype(jnp.bfloat16)
    output = lax.psum_scatter(partial_out, "lo", scatter_dimension=0, tiled=True)
    output = lax.psum_scatter(output, "tp", scatter_dimension=1, tiled=True)

    grads12, grad_taps12 = call(
        functools.partial(back_kernel, rows, tok),
        "back",
        lo,
        (grad_field, sm12, xt12, after, ahead, decay, residue, direct, taps),
        [
            down_one,
            down_two,
            down_two,
            mode_spec,
            whole((4 * edge, LANES)),
            mode_spec,
            mode_spec,
            skip_spec,
            taps_spec,
        ],
        [
            shape((lo, 2, tok, wide), jnp.bfloat16),
            shape((2, lags, rows, LANES), f32),
        ],
        [grads_spec(2), whole((2, lags, rows, LANES))],
        [padded(2), staged, states, pltpu.VMEM((2, lags, rows, LANES), f32)],
        0,
    )
    grads12 = lax.all_to_all(grads12, "lo", 0, 0, tiled=True)
    grad_taps = jnp.concatenate([grad_taps0[None], grad_taps12])
    grad_taps = jnp.sum(grad_taps.reshape(3 * lags * near, members), axis=1)
    part = jnp.concatenate([grad_skip.reshape(-1), grad_taps])
    part = jnp.pad(part, (0, -part.size % wide)).reshape(-1, wide)
    part = jnp.pad(part, ((0, -part.shape[0] % EDGE), (0, 0)))
    small = part
    for k in range(1, hi):
        small = small + lax.ppermute(part, "hi", [(z, (z + k) % hi) for z in range(hi)])
    sums.right, sums.left = tie((sums.right, sums.left), (small,))
    while sums.done < hi - 1:
        sums.step()

    reduced = sums.finish().astype(jnp.bfloat16).reshape(lo, -1, wide)
    count = reduced.shape[1]
    coarse = small.astype(jnp.bfloat16)
    fine = (small - coarse.astype(f32)).astype(jnp.bfloat16)
    extra = jnp.concatenate([coarse, fine])
    extra = jnp.broadcast_to(extra, (lo,) + extra.shape)
    reduced = jnp.concatenate([reduced, extra], axis=1)[:, None]
    reduced = lax.all_to_all(reduced, "lo", 0, 0, tiled=True)
    grad_weight = join_channels((reduced,), f32, count)[0]
    grad_streams = join_channels((grads0, grads12), grads0.dtype, tok)
    small = reduced[:, 0, count:].astype(f32)
    small = (small[:, : part.shape[0]] + small[:, part.shape[0] :]).reshape(lo, -1)
    grad_skip = small[:, :wide].reshape(channels)
    grad_short = small[:, wide : wide + 3 * lags * near].reshape(lo, 3, lags, near)
    grad_short = jnp.moveaxis(grad_short, 0, 2)
    return output, grad_streams, grad_short.reshape(3, lags, groups), grad_skip, grad_weight


def solution(mesh):
    count, parts = mesh.shape["ctx"], mesh.shape["tp"]
    lo = math.gcd(count, 8)
    cut = Mesh(mesh.devices.reshape(count // lo, lo, parts), ("hi", "lo", "tp"))
    ctx = ("hi", "lo")
    return jax.shard_map(
        shards,
        mesh=cut,
        in_specs=(
            P(None, ctx, "tp"),
            P(None, None, "tp"),
            P(None, "tp"),
            P(None, "tp"),
            P("tp"),
            P(ctx, "tp"),
            P(ctx, "tp"),
        ),
        out_specs=(
            P(ctx, "tp"),
            P(None, ctx, "tp"),
            P(None, None, "tp"),
            P("tp"),
            P(ctx, "tp"),
        ),
        check_vma=False,
    )
```

```python
import functools
import math

import jax
import jax.numpy as jnp
from jax import lax
from jax.experimental import pallas as pl
from jax.experimental.pallas import tpu as pltpu
from jax.sharding import Mesh, PartitionSpec as P

LANES = 128
EDGE = 8
STEP = 8
VMEM = 60 * 1024 * 1024


def at(token, rows):
    start = token * rows
    return pl.ds(start if isinstance(start, int) else pl.multiple_of(start, rows), rows)


def total_of(terms):
    while len(terms) > 1:
        terms = [
            terms[k] + terms[k + 1] if k + 1 < len(terms) else terms[k]
            for k in range(0, len(terms), 2)
        ]
    return terms[0]


def to_token_rows(ref, first, value, rows):
    count = value.shape[0]
    for j in range(rows):
        ref[pl.ds(first * rows + j, count, stride=rows), :] = value[
            :, j * LANES : (j + 1) * LANES
        ].astype(jnp.float32)


def fill(pad, parts, rims, rows, tok):
    first = pl.program_id(0) == 0

    @pl.when(first)
    def _():
        for i in range(pad.shape[0]):
            to_token_rows(pad.at[i], 0, rims[i], rows)

    @pl.when(jnp.logical_not(first))
    def _():
        for i in range(pad.shape[0]):
            pad[i, pl.ds(0, EDGE * rows), :] = pad[i, pl.ds(tok * rows, EDGE * rows), :]

    for i in range(pad.shape[0]):
        to_token_rows(pad.at[i], EDGE, parts[i], rows)


def rim_rows(rim_ref):
    rims = rim_ref[0].astype(jnp.float32)
    return [rims[i * EDGE : (i + 1) * EDGE] for i in range(3)]


def convolved(pad, i, taps, base, rows):
    lags = len(taps)
    window = [pad[i, at(base + EDGE - (lags - 1) + k, rows), :] for k in range(STEP + lags - 1)]
    return [
        total_of([taps[j] * window[u + lags - 1 - j] for j in range(lags)]) for u in range(STEP)
    ]


def smooth_kernel(
    rows,
    tok,
    x_ref,
    rim_ref,
    taps_ref,
    decay_ref,
    sm_ref,
    mixed_ref,
    xt_ref,
    end_ref,
    room_ref,
    pad,
    state,
):
    modes, lags = decay_ref.shape[0], taps_ref.shape[1]

    @pl.when(pl.program_id(0) == 0)
    def _():
        state[...] = jnp.zeros_like(state)

    parts = [x_ref[0, pl.ds(i * tok, tok), :] for i in range(2)]
    fill(pad, parts, rim_rows(rim_ref)[1:], rows, tok)
    for i in range(2):
        xt_ref[i] = pad[i, pl.ds(EDGE * rows, tok * rows), :]

    def smooth(n, carry):
        base = n * STEP
        results = []
        for i in range(2):
            taps = [taps_ref[i + 1, j] for j in range(lags)]
            results.append(convolved(pad, i, taps, base, rows))
            for u in range(STEP):
                sm_ref[i, at(base + u, rows), :] = results[i][u]
        for u in range(STEP):
            mixed_ref[at(base + u, rows), :] = (
                (results[0][u] * results[1][u]).astype(jnp.bfloat16).astype(jnp.float32)
            )
        return carry

    lax.fori_loop(0, tok // STEP, smooth, 0)
    decay = [decay_ref[m] for m in range(modes)]

    def advance(n, held):
        held = list(held)
        for u in range(STEP):
            x = mixed_ref[at(n * STEP + u, rows), :]
            held = [decay[m] * held[m] + x for m in range(modes)]
        return tuple(held)

    held = lax.fori_loop(0, tok // STEP, advance, tuple(state[m] for m in range(modes)))
    for m in range(modes):
        state[m] = held[m]
        end_ref[m] = held[m]


def field_kernel(
    rows,
    tok,
    x_ref,
    rim_ref,
    taps_ref,
    mixed_ref,
    before_ref,
    decay_ref,
    residue_ref,
    skip_ref,
    sm_ref,
    xt_ref,
    field_ref,
    gated_ref,
    pad,
    staged,
    state,
):
    modes, lags = decay_ref.shape[0], taps_ref.shape[1]

    @pl.when(pl.program_id(0) == 0)
    def _():
        state[...] = before_ref[...]

    fill(pad, [x_ref[0, 0]], rim_rows(rim_ref), rows, tok)
    xt_ref[...] = pad[0, pl.ds(EDGE * rows, tok * rows), :]
    taps = [taps_ref[0, j] for j in range(lags)]

    def smooth(n, carry):
        results = convolved(pad, 0, taps, n * STEP, rows)
        for u in range(STEP):
            sm_ref[at(n * STEP + u, rows), :] = results[u]
        return carry

    lax.fori_loop(0, tok // STEP, smooth, 0)
    decay = [decay_ref[m] for m in range(modes)]
    residue = [residue_ref[m] for m in range(modes)]
    skip = skip_ref[...]

    def advance(n, held):
        held = list(held)
        for u in range(STEP):
            place = at(n * STEP + u, rows)
            x = mixed_ref[place, :]
            held = [decay[m] * held[m] + x for m in range(modes)]
            field = total_of([residue[m] * held[m] for m in range(modes)] + [skip * x])
            field_ref[place, :] = field
            staged[place, :] = sm_ref[place, :] * field
        return tuple(held)

    held = lax.fori_loop(0, tok // STEP, advance, tuple(state[m] for m in range(modes)))
    for m in range(modes):
        state[m] = held[m]
    for j in range(rows):
        gated_ref[:, j * LANES : (j + 1) * LANES] = staged[
            pl.ds(j, tok, stride=rows), :
        ].astype(jnp.bfloat16)


def spread_back(
    rows, tok, i, pad, xt_at, taps, total, out_ref, gtaps_ref, staged
):
    lags = len(taps)

    def spread(n, sums):
        base = n * STEP
        sums = list(sums)
        window = [pad[i, at(base + k, rows), :] for k in range(STEP + lags - 1)]
        for u in range(STEP):
            x = xt_at(at(base + u, rows))
            for j in range(lags):
                sums[j] = sums[j] + x * window[u + j]
            staged[at(base + u, rows), :] = total_of(
                [taps[j] * window[u + j] for j in range(lags)]
            )
        return tuple(sums)

    sums = lax.fori_loop(0, tok // STEP, spread, tuple(total[i, j] for j in range(lags)))
    for j in range(lags):
        total[i, j] = sums[j]
        gtaps_ref[i, j] = sums[j]
    for j in range(rows):
        out_ref[0, i, :, j * LANES : (j + 1) * LANES] = staged[
            pl.ds(j, tok, stride=rows), :
        ].astype(jnp.bfloat16)


def cotangent_kernel(
    rows,
    tok,
    up_ref,
    sm_ref,
    mixed_ref,
    field_ref,
    decay_ref,
    heads_ref,
    hold_ref,
    grad_ref,
    zero_ref,
    ahead_ref,
    end_ref,
    gskip_ref,
    staged,
    state,
    summed,
):
    modes = decay_ref.shape[0]

    @pl.when(pl.program_id(0) == 0)
    def _():
        state[...] = jnp.zeros_like(state)
        summed[...] = jnp.zeros_like(summed)

    to_token_rows(staged, 0, up_ref[...], rows)
    decay = [decay_ref[m] for m in range(modes)]

    def retreat(n, carry):
        held, added = list(carry[:-1]), carry[-1]
        for u in range(STEP):
            place = at(tok - 1 - (n * STEP + u), rows)
            up = staged[place, :]
            grad = up * sm_ref[place, :]
            grad_ref[place, :] = grad
            zero_ref[place, :] = up * field_ref[place, :]
            added = added + grad * mixed_ref[place, :]
            held = [decay[m] * held[m] + grad for m in range(modes)]
        return tuple(held) + (added,)

    last = tok // STEP - 1
    carry = lax.fori_loop(
        0, last, retreat, tuple(state[m] for m in range(modes)) + (summed[...],)
    )
    for m in range(modes):
        ahead_ref[pl.ds(m * rows, rows), :] = carry[m]
    carry = retreat(last, carry)
    edge = EDGE * rows
    heads = [grad_ref[pl.ds(0, edge), :], heads_ref[0], heads_ref[1], zero_ref[pl.ds(0, edge), :]]
    for k, head in enumerate(heads):
        ahead_ref[pl.ds(modes * rows + k * edge, edge), :] = head
    for m in range(modes):
        state[m] = carry[m]
        end_ref[m] = carry[m]
    summed[...] = carry[-1]
    gskip_ref[...] = carry[-1]


def back_kernel(
    rows,
    tok,
    grad_ref,
    zero_ref,
    sm_ref,
    first_ref,
    xt_ref,
    after_ref,
    ahead_ref,
    decay_ref,
    residue_ref,
    skip_ref,
    taps_ref,
    out_ref,
    gtaps_ref,
    pad,
    staged,
    state,
    total,
):
    modes, lags = decay_ref.shape[0], taps_ref.shape[1]
    decay = [decay_ref[m] for m in range(modes)]
    residue = [residue_ref[m] for m in range(modes)]
    skip = skip_ref[...]

    @pl.when(pl.program_id(0) == 0)
    def _():
        total[...] = jnp.zeros_like(total)
        held = [after_ref[m] for m in range(modes)]
        for u in reversed(range(EDGE)):
            grad, one, two = [ahead_ref[at(k * EDGE + u, rows), :] for k in range(3)]
            held = [decay[m] * held[m] + grad for m in range(modes)]
            mixed = total_of([residue[m] * held[m] for m in range(modes)] + [skip * grad])
            pad[0, at(tok + u, rows), :] = ahead_ref[at(3 * EDGE + u, rows), :]
            pad[1, at(tok + u, rows), :] = mixed * two
            pad[2, at(tok + u, rows), :] = mixed * one
        for m in range(modes):
            state[m] = held[m]

    @pl.when(pl.program_id(0) != 0)
    def _():
        for i in range(3):
            pad[i, pl.ds(tok * rows, EDGE * rows), :] = pad[i, pl.ds(0, EDGE * rows), :]

    pad[0, pl.ds(0, tok * rows), :] = zero_ref[...]


    def retreat(n, held):
        held = list(held)
        for u in range(STEP):
            place = at(tok - 1 - (n * STEP + u), rows)
            grad = grad_ref[place, :]
            held = [decay[m] * held[m] + grad for m in range(modes)]
            mixed = total_of([residue[m] * held[m] for m in range(modes)] + [skip * grad])
            pad[1, place, :] = mixed * sm_ref[1, place, :]
            pad[2, place, :] = mixed * sm_ref[0, place, :]
        return tuple(held)

    held = lax.fori_loop(0, tok // STEP, retreat, tuple(state[m] for m in range(modes)))
    for m in range(modes):
        state[m] = held[m]
    for i in range(3):
        spread_back(
            rows,
            tok,
            i,
            pad,
            lambda place, i=i: xt_ref[i - 1, place, :] if i else first_ref[place, :],
            [taps_ref[i, j] for j in range(lags)],
            total,
            out_ref,
            gtaps_ref,
            staged,
        )


def whole(shape):
    return pl.BlockSpec(shape, lambda n: (0,) * len(shape))


def call(kernel, name, blocks, ins, in_specs, outs, out_specs, scratch, ops, aliases={}):
    return pl.pallas_call(
        kernel,
        grid=(blocks,),
        in_specs=in_specs,
        out_specs=out_specs,
        out_shape=outs,
        scratch_shapes=scratch,
        input_output_aliases=aliases,
        compiler_params=pltpu.CompilerParams(vmem_limit_bytes=VMEM),
        cost_estimate=pl.CostEstimate(flops=ops, bytes_accessed=0, transcendentals=0),
        name=name,
    )(*ins)


def tie_kernel(*refs):
    pass


def tie(values, after, flops=0):
    values, after = tuple(values), tuple(after)
    held = pl.BlockSpec(memory_space=pl.ANY)
    return pl.pallas_call(
        tie_kernel,
        in_specs=[held] * (len(values) + len(after)),
        out_specs=[held] * len(values),
        out_shape=[jax.ShapeDtypeStruct(a.shape, a.dtype) for a in values],
        input_output_aliases={i: i for i in range(len(values))},
        compiler_params=pltpu.CompilerParams(vmem_limit_bytes=VMEM),
        cost_estimate=pl.CostEstimate(flops=flops, bytes_accessed=0, transcendentals=0),
        name="tie",
    )(*values, *after)


def split_kernel(in_ref, out_ref):
    out_ref[0] = in_ref[...].astype(out_ref.dtype)


def split_channels(a, lo, first, count):
    tok, wide = a.shape[1], a.shape[2] // lo
    return call(
        split_kernel,
        "split",
        lo * count,
        (a,),
        [pl.BlockSpec((1, tok, wide), lambda n: (first + n // lo, 0, n % lo))],
        jax.ShapeDtypeStruct((lo, count, tok, wide), a.dtype),
        pl.BlockSpec((1, 1, tok, wide), lambda n: (n % lo, n // lo, 0, 0)),
        [],
        0,
    )


def pack_kernel(tok, x_ref, rim_ref, out_ref, first_ref):
    first_ref[0, 0] = x_ref[0]
    out_ref[0, pl.ds(0, tok), :] = x_ref[1]
    out_ref[0, pl.ds(tok, tok), :] = x_ref[2]
    rims = [rim_ref[i].astype(jnp.float32) for i in range(3)]
    rims.append(jnp.zeros_like(rims[0]))
    out_ref[0, pl.ds(2 * tok, 4 * EDGE), :] = jnp.concatenate(rims).astype(out_ref.dtype)


def pack(streams, rim, lo):
    tok, wide = streams.shape[1], streams.shape[2] // lo
    held = 2 * tok + 4 * EDGE
    return call(
        functools.partial(pack_kernel, tok),
        "pack",
        lo,
        (streams, rim),
        [
            pl.BlockSpec((3, tok, wide), lambda n: (0, 0, n)),
            pl.BlockSpec((3, EDGE, wide), lambda n: (0, 0, n)),
        ],
        [
            jax.ShapeDtypeStruct((lo, held, wide), streams.dtype),
            jax.ShapeDtypeStruct((lo, 1, tok, wide), streams.dtype),
        ],
        [
            pl.BlockSpec((1, held, wide), lambda n: (n, 0, 0)),
            pl.BlockSpec((1, 1, tok, wide), lambda n: (n, 0, 0, 0)),
        ],
        [],
        0,
    )


def join_kernel(*refs):
    out_ref, first = refs[-1], 0
    for ref in refs[:-1]:
        out_ref[pl.ds(first, ref.shape[1])] = ref[0].astype(out_ref.dtype)
        first += ref.shape[1]


def join_channels(pieces, dtype, tok):
    lo, _, _, wide = pieces[0].shape
    total = sum(piece.shape[1] for piece in pieces)
    return call(
        join_kernel,
        "join",
        lo,
        pieces,
        [
            pl.BlockSpec((1, piece.shape[1], tok, wide), lambda n: (n, 0, 0, 0))
            for piece in pieces
        ],
        jax.ShapeDtypeStruct((total, tok, lo * wide), dtype),
        pl.BlockSpec((total, tok, wide), lambda n: (0, 0, n)),
        [],
        0,
    )


def project_kernel(x_ref, w_ref, out_ref):
    out_ref[...] = lax.dot_general(
        x_ref[...], w_ref[...], (((1,), (1,)), ((), ())), preferred_element_type=jnp.float32
    ).astype(out_ref.dtype)


def project(x, w):
    (tokens, wide), outs = x.shape, w.shape[0]
    size = math.gcd(outs, 512)
    return call(
        project_kernel,
        "project",
        outs // size,
        (x, w),
        [whole((tokens, wide)), pl.BlockSpec((size, wide), lambda n: (n, 0))],
        jax.ShapeDtypeStruct((tokens, outs), x.dtype),
        pl.BlockSpec((tokens, size), lambda n: (0, n)),
        [],
        0,
    )


class Planes:
    def __init__(self, block, hi, plane):
        self.block, self.hi, self.plane = block, hi, plane
        self.rows, self.done, self.placed = block.shape[0], 0, 0
        self.right, self.left = block, block
        self.arrived = []
        self.result = None

    def step(self):
        self.done += 1
        k, hi = self.done, self.hi
        self.right = lax.ppermute(self.right, "hi", [(z, z + 1) for z in range(k - 1, hi - 1)])
        self.left = lax.ppermute(self.left, "hi", [(z + 1, z) for z in range(hi - k)])
        self.arrived.append((self.right, self.left))

    def put(self, piece, there):
        valid = jnp.logical_and(there >= 0, there < self.hi)
        self.result = lax.dynamic_update_slice_in_dim(
            self.result,
            jnp.where(valid, piece, self.block),
            jnp.where(valid, there, self.plane) * self.rows,
            0,
        )

    def place(self):
        if not self.placed:
            self.put(self.block, self.plane)
        if self.done:
            self.arrived[-1] = (self.right, self.left)
        while self.placed < self.done:
            self.placed += 1
            k, (right, left) = self.placed, self.arrived[self.placed - 1]
            if 2 * k < self.hi:
                self.put(right, self.plane - k)
                self.put(left, self.plane + k)
            else:
                below = self.plane >= k
                self.put(
                    jnp.where(below, right, left),
                    jnp.where(below, self.plane - k, self.plane + k),
                )


class Sums:
    def __init__(self, partial, hi, plane):
        self.partial, self.hi, self.plane = partial, hi, plane
        self.rows, self.done = partial.shape[0] // hi, 0
        self.right, self.left = None, None

    def part(self, d):
        first = jnp.clip(d, 0, self.hi - 1) * self.rows
        return lax.dynamic_slice_in_dim(self.partial, first, self.rows, 0).astype(jnp.float32)

    def step(self):
        self.done += 1
        s, hi, dtype = self.done, self.hi, self.partial.dtype
        self.to_right = add(self.part(hi - s + self.plane), self.right).astype(dtype)
        self.to_left = add(self.part(s - hi + self.plane), self.left).astype(dtype)
        self.right = lax.ppermute(self.to_right, "hi", [(z, z + 1) for z in range(s)])
        self.left = lax.ppermute(
            self.to_left, "hi", [(hi - 1 - z, hi - 2 - z) for z in range(s)]
        )

    def finish(self):
        return add(add(self.part(self.plane), self.right), self.left)


def add(mine, arrived):
    return mine if arrived is None else mine + arrived.astype(jnp.float32)


def shards(streams, short_filter, residues, rates, skip, out_weight, out_cotangent):
    hi, lo = lax.axis_size("hi"), lax.axis_size("lo")
    plane, place = lax.axis_index("hi"), lax.axis_index("lo")
    tok, channels = streams.shape[1:]
    modes, groups = residues.shape
    members = channels // groups
    lags = short_filter.shape[1]
    wide, near = channels // lo, groups // lo
    rows = wide // LANES
    length = tok * lo
    f32 = jnp.float32
    shape = jax.ShapeDtypeStruct

    def mine(a):
        a = lax.dynamic_slice_in_dim(a, place * near, near, a.ndim - 1)
        return jnp.repeat(a, members, axis=-1).reshape(a.shape[:-1] + (rows, LANES))

    taps, residue, rate = mine(short_filter), mine(residues), mine(rates)
    decay = jnp.exp(-rate)
    plane_decay = jnp.exp(-rate * length)
    direct = lax.dynamic_slice_in_dim(skip, place * wide, wide, 0).reshape(rows, LANES)

    ends = [(z * lo - 1, z * lo) for z in range(1, hi)]
    rim = lax.ppermute(streams[:, tok - EDGE :, :], ("hi", "lo"), ends)
    own = lax.all_to_all(split_channels(out_weight[None], lo, 0, 1), "lo", 0, 0, tiled=True)
    own = own.reshape(-1, wide)
    packed12, packed0 = tie(pack(streams, rim, lo), (own,))
    x12 = lax.all_to_all(packed12, "lo", 0, 0, tiled=True)
    (packed0,) = tie((packed0,), (x12,))
    x0 = lax.all_to_all(packed0, "lo", 0, 0, tiled=True)
    flat = tok * rows
    tokens = length * rows
    up_one = pl.BlockSpec((flat, LANES), lambda n: (n, 0))
    up_two = pl.BlockSpec((2, flat, LANES), lambda n: (0, n, 0))
    up_wide = pl.BlockSpec((tok, wide), lambda n: (n, 0))
    down_one = pl.BlockSpec((flat, LANES), lambda n: (lo - 1 - n, 0))
    down_two = pl.BlockSpec((2, flat, LANES), lambda n: (0, lo - 1 - n, 0))
    down_wide = pl.BlockSpec((tok, wide), lambda n: (lo - 1 - n, 0))
    taps_spec = whole((3, lags, rows, LANES))
    mode_spec = whole((modes, rows, LANES))
    skip_spec = whole((rows, LANES))
    held_spec = pl.BlockSpec(memory_space=pl.ANY)
    states = pltpu.VMEM((modes, rows, LANES), f32)
    staged = pltpu.VMEM((flat, LANES), f32)
    work = length * wide

    def padded(count):
        return pltpu.VMEM((count, (tok + EDGE) * rows, LANES), f32)

    rim_spec = pl.BlockSpec((1, 4 * EDGE, wide), lambda n: (0, 2 * tok // (4 * EDGE), 0))

    def grads_spec(count):
        return pl.BlockSpec((1, count, tok, wide), lambda n: (lo - 1 - n, 0, 0, 0))

    mover = Planes(own, hi, plane)
    mover.step()
    (cotangent,) = tie((out_cotangent,), (x12, mover.right, mover.left))
    cotangent = lax.all_gather(cotangent, "tp", axis=1, tiled=True)
    cotangent = lax.all_gather(cotangent, "lo", axis=0, tiled=True)

    sm12, mixed, xt12, ending, mover.result = call(
        functools.partial(smooth_kernel, rows, tok),
        "smooth",
        lo,
        (x12, x12, taps, decay),
        [
            pl.BlockSpec((1, 2 * tok, wide), lambda n: (n, 0, 0)),
            rim_spec,
            taps_spec,
            mode_spec,
        ],
        [
            shape((2, tokens, LANES), f32),
            shape((tokens, LANES), f32),
            shape((2, tokens, LANES), f32),
            shape((modes, rows, LANES), f32),
            shape((hi * own.shape[0], wide), own.dtype),
        ],
        [up_two, up_one, up_two, mode_spec, held_spec],
        [padded(2), states],
        0,
    )
    mover.step()

    def from_plane(a, distance):
        pairs = [(z + distance, z) for z in range(max(0, -distance), hi - max(0, distance))]
        return lax.ppermute(a, "hi", pairs)

    before = jnp.zeros_like(ending)
    for k in reversed(range(1, hi)):
        before = from_plane(ending, -k) + plane_decay * before
    mover.right, mover.left = tie((mover.right, mover.left), (before,))
    sm0, xt0, field, gated = call(
        functools.partial(field_kernel, rows, tok),
        "field",
        lo,
        (x0, x12, taps, mixed, before, decay, residue, direct),
        [
            pl.BlockSpec((1, 1, tok, wide), lambda n: (n, 0, 0, 0)),
            rim_spec,
            taps_spec,
            up_one,
            mode_spec,
            mode_spec,
            mode_spec,
            skip_spec,
        ],
        [
            shape((tokens, LANES), f32),
            shape((tokens, LANES), f32),
            shape((tokens, LANES), f32),
            shape((length, wide), jnp.bfloat16),
        ],
        [up_one, up_one, up_one, up_wide],
        [padded(1), staged, states],
        0,
    )
    mover.place()
    while mover.done < hi - 1:
        mover.step()

    partial_grad = lax.dot_general(
        cotangent, gated, (((0,), (0,)), ((), ())), preferred_element_type=f32
    ).astype(jnp.bfloat16)
    sums = Sums(partial_grad, hi, plane)
    sums.step()
    mover.right, mover.left = tie((mover.right, mover.left), (sums.to_right, sums.to_left))
    mover.place()
    weights = mover.result

    upstream = jnp.dot(cotangent, weights, preferred_element_type=f32)
    partial_out = project(gated, weights)
    output = lax.psum_scatter(partial_out, "lo", scatter_dimension=0, tiled=True)
    output = lax.psum_scatter(output, "tp", scatter_dimension=1, tiled=True)
    edge = EDGE * rows
    held = modes * rows + 4 * edge
    grad_field, grad_zero, ahead, back_end, grad_skip = call(
        functools.partial(cotangent_kernel, rows, tok),
        "cotangent",
        lo,
        (upstream, sm0, mixed, field, decay, sm12, partial_out),
        [
            down_wide,
            down_one,
            down_one,
            down_one,
            mode_spec,
            whole((2, edge, LANES)),
            held_spec,
        ],
        [
            shape((tokens, LANES), f32),
            shape((tokens, LANES), f32),
            shape((held, LANES), f32),
            shape((modes, rows, LANES), f32),
            shape((rows, LANES), f32),
        ],
        [down_one, down_one, whole((held, LANES)), mode_spec, skip_spec],
        [staged, states, pltpu.VMEM((rows, LANES), f32)],
        0,
    )

    ahead, back_end = tie((ahead, back_end), (sums.right, sums.left))
    ahead = from_plane(ahead, 1)
    beyond = jnp.zeros_like(back_end)
    for k in reversed(range(2, hi)):
        beyond = from_plane(back_end, k) + plane_decay * beyond
    after = ahead[: modes * rows].reshape(back_end.shape) + beyond * jnp.exp(
        -rate * (length - EDGE)
    )
    ahead = ahead[modes * rows :]

    sums.right, sums.left = tie((sums.right, sums.left), (after, ahead))
    sums.step()
    grads, grad_taps = call(
        functools.partial(back_kernel, rows, tok),
        "back",
        lo,
        (grad_field, grad_zero, sm12, xt0, xt12, after, ahead, decay, residue, direct, taps),
        [
            down_one,
            down_one,
            down_two,
            down_one,
            down_two,
            mode_spec,
            whole((4 * edge, LANES)),
            mode_spec,
            mode_spec,
            skip_spec,
            taps_spec,
        ],
        [
            shape((lo, 3, tok, wide), jnp.bfloat16),
            shape((3, lags, rows, LANES), f32),
        ],
        [grads_spec(3), taps_spec],
        [padded(3), staged, states, pltpu.VMEM((3, lags, rows, LANES), f32)],
        0,
    )
    grads = lax.all_to_all(grads, "lo", 0, 0, tiled=True)
    sums.right, sums.left = tie((sums.right, sums.left), (grad_taps,), 30 * 10**9)
    grad_taps = jnp.sum(grad_taps.reshape(3 * lags * near, members), axis=1)
    part = jnp.concatenate([grad_skip.reshape(-1), grad_taps])
    part = jnp.pad(part, (0, -part.size % wide)).reshape(-1, wide)
    part = jnp.pad(part, ((0, -part.shape[0] % EDGE), (0, 0)))
    small = part
    for k in range(1, hi):
        small = small + lax.ppermute(part, "hi", [(z, (z + k) % hi) for z in range(hi)])
    while sums.done < hi - 1:
        sums.step()

    reduced = sums.finish().astype(jnp.bfloat16).reshape(lo, -1, wide)
    count = reduced.shape[1]
    coarse = small.astype(jnp.bfloat16)
    fine = (small - coarse.astype(f32)).astype(jnp.bfloat16)
    extra = jnp.concatenate([coarse, fine])
    extra = jnp.broadcast_to(extra, (lo,) + extra.shape)
    reduced = jnp.concatenate([reduced, extra], axis=1)[:, None]
    (reduced,) = tie((reduced,), (output,), 30 * 10**9)
    reduced = lax.all_to_all(reduced, "lo", 0, 0, tiled=True)
    grad_weight = join_channels((reduced,), f32, count)[0]
    grad_streams = join_channels((grads,), grads.dtype, tok)
    small = reduced[:, 0, count:].astype(f32)
    small = (small[:, : part.shape[0]] + small[:, part.shape[0] :]).reshape(lo, -1)
    grad_skip = small[:, :wide].reshape(channels)
    grad_short = small[:, wide : wide + 3 * lags * near].reshape(lo, 3, lags, near)
    grad_short = jnp.moveaxis(grad_short, 0, 2)
    return output, grad_streams, grad_short.reshape(3, lags, groups), grad_skip, grad_weight


def solution(mesh):
    count, parts = mesh.shape["ctx"], mesh.shape["tp"]
    lo = math.gcd(count, 8)
    cut = Mesh(mesh.devices.reshape(count // lo, lo, parts), ("hi", "lo", "tp"))
    ctx = ("hi", "lo")
    return jax.shard_map(
        shards,
        mesh=cut,
        in_specs=(
            P(None, ctx, "tp"),
            P(None, None, "tp"),
            P(None, "tp"),
            P(None, "tp"),
            P("tp"),
            P(ctx, "tp"),
            P(ctx, "tp"),
        ),
        out_specs=(
            P(ctx, "tp"),
            P(None, ctx, "tp"),
            P(None, None, "tp"),
            P("tp"),
            P(ctx, "tp"),
        ),
        check_vma=False,
    )
```

```python
import functools
import math

import jax
import jax.numpy as jnp
from jax import lax
from jax.experimental import pallas as pl
from jax.experimental.pallas import tpu as pltpu
from jax.sharding import Mesh, PartitionSpec as P

LANES = 128
EDGE = 8
STEP = 8
VMEM = 60 * 1024 * 1024


def at(token, rows):
    start = token * rows
    return pl.ds(start if isinstance(start, int) else pl.multiple_of(start, rows), rows)


def total_of(terms):
    while len(terms) > 1:
        terms = [
            terms[k] + terms[k + 1] if k + 1 < len(terms) else terms[k]
            for k in range(0, len(terms), 2)
        ]
    return terms[0]


def to_token_rows(ref, first, value, rows):
    count = value.shape[0]
    for j in range(rows):
        ref[pl.ds(first * rows + j, count, stride=rows), :] = value[
            :, j * LANES : (j + 1) * LANES
        ].astype(jnp.float32)


def fill(pad, parts, rims, rows, tok):
    first = pl.program_id(0) == 0

    @pl.when(first)
    def _():
        for i in range(pad.shape[0]):
            to_token_rows(pad.at[i], 0, rims[i], rows)

    @pl.when(jnp.logical_not(first))
    def _():
        for i in range(pad.shape[0]):
            pad[i, pl.ds(0, EDGE * rows), :] = pad[i, pl.ds(tok * rows, EDGE * rows), :]

    for i in range(pad.shape[0]):
        to_token_rows(pad.at[i], EDGE, parts[i], rows)


def rim_rows(rim_ref):
    rims = rim_ref[0].astype(jnp.float32)
    return [rims[i * EDGE : (i + 1) * EDGE] for i in range(3)]


def convolved(pad, i, taps, base, rows):
    lags = len(taps)
    window = [pad[i, at(base + EDGE - (lags - 1) + k, rows), :] for k in range(STEP + lags - 1)]
    return [
        total_of([taps[j] * window[u + lags - 1 - j] for j in range(lags)]) for u in range(STEP)
    ]


def smooth_kernel(
    rows,
    tok,
    x_ref,
    rim_ref,
    taps_ref,
    decay_ref,
    sm_ref,
    mixed_ref,
    xt_ref,
    end_ref,
    room_ref,
    pad,
    state,
):
    modes, lags = decay_ref.shape[0], taps_ref.shape[1]

    @pl.when(pl.program_id(0) == 0)
    def _():
        state[...] = jnp.zeros_like(state)

    parts = [x_ref[0, pl.ds(i * tok, tok), :] for i in range(2)]
    fill(pad, parts, rim_rows(rim_ref)[1:], rows, tok)
    for i in range(2):
        xt_ref[i] = pad[i, pl.ds(EDGE * rows, tok * rows), :]

    def smooth(n, carry):
        base = n * STEP
        results = []
        for i in range(2):
            taps = [taps_ref[i + 1, j] for j in range(lags)]
            results.append(convolved(pad, i, taps, base, rows))
            for u in range(STEP):
                sm_ref[i, at(base + u, rows), :] = results[i][u]
        for u in range(STEP):
            mixed_ref[at(base + u, rows), :] = (
                (results[0][u] * results[1][u]).astype(jnp.bfloat16).astype(jnp.float32)
            )
        return carry

    lax.fori_loop(0, tok // STEP, smooth, 0)
    decay = [decay_ref[m] for m in range(modes)]

    def advance(n, held):
        held = list(held)
        for u in range(STEP):
            x = mixed_ref[at(n * STEP + u, rows), :]
            held = [decay[m] * held[m] + x for m in range(modes)]
        return tuple(held)

    held = lax.fori_loop(0, tok // STEP, advance, tuple(state[m] for m in range(modes)))
    for m in range(modes):
        state[m] = held[m]
        end_ref[m] = held[m]


def field_kernel(
    rows,
    tok,
    x_ref,
    rim_ref,
    taps_ref,
    mixed_ref,
    before_ref,
    decay_ref,
    residue_ref,
    skip_ref,
    sm_ref,
    xt_ref,
    field_ref,
    gated_ref,
    pad,
    staged,
    state,
):
    modes, lags = decay_ref.shape[0], taps_ref.shape[1]

    @pl.when(pl.program_id(0) == 0)
    def _():
        state[...] = before_ref[...]

    fill(pad, [x_ref[0, 0]], rim_rows(rim_ref), rows, tok)
    xt_ref[...] = pad[0, pl.ds(EDGE * rows, tok * rows), :]
    taps = [taps_ref[0, j] for j in range(lags)]

    def smooth(n, carry):
        results = convolved(pad, 0, taps, n * STEP, rows)
        for u in range(STEP):
            sm_ref[at(n * STEP + u, rows), :] = results[u]
        return carry

    lax.fori_loop(0, tok // STEP, smooth, 0)
    decay = [decay_ref[m] for m in range(modes)]
    residue = [residue_ref[m] for m in range(modes)]
    skip = skip_ref[...]

    def advance(n, held):
        held = list(held)
        for u in range(STEP):
            place = at(n * STEP + u, rows)
            x = mixed_ref[place, :]
            held = [decay[m] * held[m] + x for m in range(modes)]
            field = total_of([residue[m] * held[m] for m in range(modes)] + [skip * x])
            field_ref[place, :] = field
            staged[place, :] = sm_ref[place, :] * field
        return tuple(held)

    held = lax.fori_loop(0, tok // STEP, advance, tuple(state[m] for m in range(modes)))
    for m in range(modes):
        state[m] = held[m]
    for j in range(rows):
        gated_ref[:, j * LANES : (j + 1) * LANES] = staged[
            pl.ds(j, tok, stride=rows), :
        ].astype(jnp.bfloat16)


def spread_back(
    rows, tok, i, pad, xt_at, taps, total, out_ref, gtaps_ref, staged
):
    lags = len(taps)

    def spread(n, sums):
        base = n * STEP
        sums = list(sums)
        window = [pad[i, at(base + k, rows), :] for k in range(STEP + lags - 1)]
        for u in range(STEP):
            x = xt_at(at(base + u, rows))
            for j in range(lags):
                sums[j] = sums[j] + x * window[u + j]
            staged[at(base + u, rows), :] = total_of(
                [taps[j] * window[u + j] for j in range(lags)]
            )
        return tuple(sums)

    sums = lax.fori_loop(0, tok // STEP, spread, tuple(total[i, j] for j in range(lags)))
    for j in range(lags):
        total[i, j] = sums[j]
        gtaps_ref[i, j] = sums[j]
    for j in range(rows):
        out_ref[0, i, :, j * LANES : (j + 1) * LANES] = staged[
            pl.ds(j, tok, stride=rows), :
        ].astype(jnp.bfloat16)


def cotangent_kernel(
    rows,
    tok,
    up_ref,
    sm_ref,
    mixed_ref,
    field_ref,
    decay_ref,
    heads_ref,
    hold_ref,
    grad_ref,
    zero_ref,
    ahead_ref,
    end_ref,
    gskip_ref,
    staged,
    state,
    summed,
):
    modes = decay_ref.shape[0]

    @pl.when(pl.program_id(0) == 0)
    def _():
        state[...] = jnp.zeros_like(state)
        summed[...] = jnp.zeros_like(summed)

    to_token_rows(staged, 0, up_ref[...], rows)
    decay = [decay_ref[m] for m in range(modes)]

    def retreat(n, carry):
        held, added = list(carry[:-1]), carry[-1]
        for u in range(STEP):
            place = at(tok - 1 - (n * STEP + u), rows)
            up = staged[place, :]
            grad = up * sm_ref[place, :]
            grad_ref[place, :] = grad
            zero_ref[place, :] = up * field_ref[place, :]
            added = added + grad * mixed_ref[place, :]
            held = [decay[m] * held[m] + grad for m in range(modes)]
        return tuple(held) + (added,)

    last = tok // STEP - 1
    carry = lax.fori_loop(
        0, last, retreat, tuple(state[m] for m in range(modes)) + (summed[...],)
    )
    for m in range(modes):
        ahead_ref[pl.ds(m * rows, rows), :] = carry[m]
    carry = retreat(last, carry)
    edge = EDGE * rows
    heads = [grad_ref[pl.ds(0, edge), :], heads_ref[0], heads_ref[1], zero_ref[pl.ds(0, edge), :]]
    for k, head in enumerate(heads):
        ahead_ref[pl.ds(modes * rows + k * edge, edge), :] = head
    for m in range(modes):
        state[m] = carry[m]
        end_ref[m] = carry[m]
    summed[...] = carry[-1]
    gskip_ref[...] = carry[-1]


def back_kernel(
    rows,
    tok,
    grad_ref,
    zero_ref,
    sm_ref,
    first_ref,
    xt_ref,
    after_ref,
    ahead_ref,
    decay_ref,
    residue_ref,
    skip_ref,
    taps_ref,
    out_ref,
    gtaps_ref,
    pad,
    staged,
    state,
    total,
):
    modes, lags = decay_ref.shape[0], taps_ref.shape[1]
    decay = [decay_ref[m] for m in range(modes)]
    residue = [residue_ref[m] for m in range(modes)]
    skip = skip_ref[...]

    @pl.when(pl.program_id(0) == 0)
    def _():
        total[...] = jnp.zeros_like(total)
        held = [after_ref[m] for m in range(modes)]
        for u in reversed(range(EDGE)):
            grad, one, two = [ahead_ref[at(k * EDGE + u, rows), :] for k in range(3)]
            held = [decay[m] * held[m] + grad for m in range(modes)]
            mixed = total_of([residue[m] * held[m] for m in range(modes)] + [skip * grad])
            pad[0, at(tok + u, rows), :] = ahead_ref[at(3 * EDGE + u, rows), :]
            pad[1, at(tok + u, rows), :] = mixed * two
            pad[2, at(tok + u, rows), :] = mixed * one
        for m in range(modes):
            state[m] = held[m]

    @pl.when(pl.program_id(0) != 0)
    def _():
        for i in range(3):
            pad[i, pl.ds(tok * rows, EDGE * rows), :] = pad[i, pl.ds(0, EDGE * rows), :]

    pad[0, pl.ds(0, tok * rows), :] = zero_ref[...]


    def retreat(n, held):
        held = list(held)
        for u in range(STEP):
            place = at(tok - 1 - (n * STEP + u), rows)
            grad = grad_ref[place, :]
            held = [decay[m] * held[m] + grad for m in range(modes)]
            mixed = total_of([residue[m] * held[m] for m in range(modes)] + [skip * grad])
            pad[1, place, :] = mixed * sm_ref[1, place, :]
            pad[2, place, :] = mixed * sm_ref[0, place, :]
        return tuple(held)

    held = lax.fori_loop(0, tok // STEP, retreat, tuple(state[m] for m in range(modes)))
    for m in range(modes):
        state[m] = held[m]
    for i in range(3):
        spread_back(
            rows,
            tok,
            i,
            pad,
            lambda place, i=i: xt_ref[i - 1, place, :] if i else first_ref[place, :],
            [taps_ref[i, j] for j in range(lags)],
            total,
            out_ref,
            gtaps_ref,
            staged,
        )


def whole(shape):
    return pl.BlockSpec(shape, lambda n: (0,) * len(shape))


def call(kernel, name, blocks, ins, in_specs, outs, out_specs, scratch, ops, aliases={}):
    return pl.pallas_call(
        kernel,
        grid=(blocks,),
        in_specs=in_specs,
        out_specs=out_specs,
        out_shape=outs,
        scratch_shapes=scratch,
        input_output_aliases=aliases,
        compiler_params=pltpu.CompilerParams(vmem_limit_bytes=VMEM),
        cost_estimate=pl.CostEstimate(flops=ops, bytes_accessed=0, transcendentals=0),
        name=name,
    )(*ins)


def tie_kernel(*refs):
    pass


def tie(values, after, flops=0):
    values, after = tuple(values), tuple(after)
    held = pl.BlockSpec(memory_space=pl.ANY)
    return pl.pallas_call(
        tie_kernel,
        in_specs=[held] * (len(values) + len(after)),
        out_specs=[held] * len(values),
        out_shape=[jax.ShapeDtypeStruct(a.shape, a.dtype) for a in values],
        input_output_aliases={i: i for i in range(len(values))},
        compiler_params=pltpu.CompilerParams(vmem_limit_bytes=VMEM),
        cost_estimate=pl.CostEstimate(flops=flops, bytes_accessed=0, transcendentals=0),
        name="tie",
    )(*values, *after)


def split_kernel(in_ref, out_ref):
    out_ref[0] = in_ref[...].astype(out_ref.dtype)


def split_channels(a, lo, first, count):
    tok, wide = a.shape[1], a.shape[2] // lo
    return call(
        split_kernel,
        "split",
        lo * count,
        (a,),
        [pl.BlockSpec((1, tok, wide), lambda n: (first + n // lo, 0, n % lo))],
        jax.ShapeDtypeStruct((lo, count, tok, wide), a.dtype),
        pl.BlockSpec((1, 1, tok, wide), lambda n: (n % lo, n // lo, 0, 0)),
        [],
        0,
    )


def pack_kernel(tok, x_ref, rim_ref, out_ref, first_ref):
    first_ref[0, 0] = x_ref[0]
    out_ref[0, pl.ds(0, tok), :] = x_ref[1]
    out_ref[0, pl.ds(tok, tok), :] = x_ref[2]
    rims = [rim_ref[i].astype(jnp.float32) for i in range(3)]
    rims.append(jnp.zeros_like(rims[0]))
    out_ref[0, pl.ds(2 * tok, 4 * EDGE), :] = jnp.concatenate(rims).astype(out_ref.dtype)


def pack(streams, rim, lo):
    tok, wide = streams.shape[1], streams.shape[2] // lo
    held = 2 * tok + 4 * EDGE
    return call(
        functools.partial(pack_kernel, tok),
        "pack",
        lo,
        (streams, rim),
        [
            pl.BlockSpec((3, tok, wide), lambda n: (0, 0, n)),
            pl.BlockSpec((3, EDGE, wide), lambda n: (0, 0, n)),
        ],
        [
            jax.ShapeDtypeStruct((lo, held, wide), streams.dtype),
            jax.ShapeDtypeStruct((lo, 1, tok, wide), streams.dtype),
        ],
        [
            pl.BlockSpec((1, held, wide), lambda n: (n, 0, 0)),
            pl.BlockSpec((1, 1, tok, wide), lambda n: (n, 0, 0, 0)),
        ],
        [],
        0,
    )


def join_kernel(*refs):
    out_ref, first = refs[-1], 0
    for ref in refs[:-1]:
        out_ref[pl.ds(first, ref.shape[1])] = ref[0].astype(out_ref.dtype)
        first += ref.shape[1]


def join_channels(pieces, dtype, tok):
    lo, _, _, wide = pieces[0].shape
    total = sum(piece.shape[1] for piece in pieces)
    return call(
        join_kernel,
        "join",
        lo,
        pieces,
        [
            pl.BlockSpec((1, piece.shape[1], tok, wide), lambda n: (n, 0, 0, 0))
            for piece in pieces
        ],
        jax.ShapeDtypeStruct((total, tok, lo * wide), dtype),
        pl.BlockSpec((total, tok, wide), lambda n: (0, 0, n)),
        [],
        0,
    )


def project_kernel(x_ref, w_ref, out_ref):
    out_ref[...] = lax.dot_general(
        x_ref[...], w_ref[...], (((1,), (1,)), ((), ())), preferred_element_type=jnp.float32
    ).astype(out_ref.dtype)


def project(x, w):
    (tokens, wide), outs = x.shape, w.shape[0]
    size = math.gcd(outs, 512)
    return call(
        project_kernel,
        "project",
        outs // size,
        (x, w),
        [whole((tokens, wide)), pl.BlockSpec((size, wide), lambda n: (n, 0))],
        jax.ShapeDtypeStruct((tokens, outs), x.dtype),
        pl.BlockSpec((tokens, size), lambda n: (0, n)),
        [],
        0,
    )


class Planes:
    def __init__(self, block, hi, plane):
        self.block, self.hi, self.plane = block, hi, plane
        self.rows, self.done, self.placed = block.shape[0], 0, 0
        self.right, self.left = block, block
        self.arrived = []
        self.result = None

    def step(self):
        self.done += 1
        k, hi = self.done, self.hi
        self.right = lax.ppermute(self.right, "hi", [(z, z + 1) for z in range(k - 1, hi - 1)])
        self.left = lax.ppermute(self.left, "hi", [(z + 1, z) for z in range(hi - k)])
        self.arrived.append((self.right, self.left))

    def put(self, piece, there):
        valid = jnp.logical_and(there >= 0, there < self.hi)
        self.result = lax.dynamic_update_slice_in_dim(
            self.result,
            jnp.where(valid, piece, self.block),
            jnp.where(valid, there, self.plane) * self.rows,
            0,
        )

    def place(self):
        if not self.placed:
            self.put(self.block, self.plane)
        if self.done:
            self.arrived[-1] = (self.right, self.left)
        while self.placed < self.done:
            self.placed += 1
            k, (right, left) = self.placed, self.arrived[self.placed - 1]
            if 2 * k < self.hi:
                self.put(right, self.plane - k)
                self.put(left, self.plane + k)
            else:
                below = self.plane >= k
                self.put(
                    jnp.where(below, right, left),
                    jnp.where(below, self.plane - k, self.plane + k),
                )


class Sums:
    def __init__(self, partial, hi, plane):
        self.partial, self.hi, self.plane = partial, hi, plane
        self.rows, self.done = partial.shape[0] // hi, 0
        self.right, self.left = None, None

    def part(self, d):
        first = jnp.clip(d, 0, self.hi - 1) * self.rows
        return lax.dynamic_slice_in_dim(self.partial, first, self.rows, 0).astype(jnp.float32)

    def step(self):
        self.done += 1
        s, hi, dtype = self.done, self.hi, self.partial.dtype
        self.to_right = add(self.part(hi - s + self.plane), self.right).astype(dtype)
        self.to_left = add(self.part(s - hi + self.plane), self.left).astype(dtype)
        self.right = lax.ppermute(self.to_right, "hi", [(z, z + 1) for z in range(s)])
        self.left = lax.ppermute(
            self.to_left, "hi", [(hi - 1 - z, hi - 2 - z) for z in range(s)]
        )

    def finish(self):
        return add(add(self.part(self.plane), self.right), self.left)


def add(mine, arrived):
    return mine if arrived is None else mine + arrived.astype(jnp.float32)


def shards(streams, short_filter, residues, rates, skip, out_weight, out_cotangent):
    hi, lo = lax.axis_size("hi"), lax.axis_size("lo")
    plane, place = lax.axis_index("hi"), lax.axis_index("lo")
    tok, channels = streams.shape[1:]
    modes, groups = residues.shape
    members = channels // groups
    lags = short_filter.shape[1]
    wide, near = channels // lo, groups // lo
    rows = wide // LANES
    length = tok * lo
    f32 = jnp.float32
    shape = jax.ShapeDtypeStruct

    def mine(a):
        a = lax.dynamic_slice_in_dim(a, place * near, near, a.ndim - 1)
        return jnp.repeat(a, members, axis=-1).reshape(a.shape[:-1] + (rows, LANES))

    taps, residue, rate = mine(short_filter), mine(residues), mine(rates)
    decay = jnp.exp(-rate)
    plane_decay = jnp.exp(-rate * length)
    direct = lax.dynamic_slice_in_dim(skip, place * wide, wide, 0).reshape(rows, LANES)

    ends = [(z * lo - 1, z * lo) for z in range(1, hi)]
    rim = lax.ppermute(streams[:, tok - EDGE :, :], ("hi", "lo"), ends)
    own = lax.all_to_all(split_channels(out_weight[None], lo, 0, 1), "lo", 0, 0, tiled=True)
    own = own.reshape(-1, wide)
    packed12, packed0 = tie(pack(streams, rim, lo), (own,))
    x12 = lax.all_to_all(packed12, "lo", 0, 0, tiled=True)
    (packed0,) = tie((packed0,), (x12,))
    x0 = lax.all_to_all(packed0, "lo", 0, 0, tiled=True)
    flat = tok * rows
    tokens = length * rows
    up_one = pl.BlockSpec((flat, LANES), lambda n: (n, 0))
    up_two = pl.BlockSpec((2, flat, LANES), lambda n: (0, n, 0))
    up_wide = pl.BlockSpec((tok, wide), lambda n: (n, 0))
    down_one = pl.BlockSpec((flat, LANES), lambda n: (lo - 1 - n, 0))
    down_two = pl.BlockSpec((2, flat, LANES), lambda n: (0, lo - 1 - n, 0))
    down_wide = pl.BlockSpec((tok, wide), lambda n: (lo - 1 - n, 0))
    taps_spec = whole((3, lags, rows, LANES))
    mode_spec = whole((modes, rows, LANES))
    skip_spec = whole((rows, LANES))
    held_spec = pl.BlockSpec(memory_space=pl.ANY)
    states = pltpu.VMEM((modes, rows, LANES), f32)
    staged = pltpu.VMEM((flat, LANES), f32)
    work = length * wide

    def padded(count):
        return pltpu.VMEM((count, (tok + EDGE) * rows, LANES), f32)

    rim_spec = pl.BlockSpec((1, 4 * EDGE, wide), lambda n: (0, 2 * tok // (4 * EDGE), 0))

    def grads_spec(count):
        return pl.BlockSpec((1, count, tok, wide), lambda n: (lo - 1 - n, 0, 0, 0))

    mover = Planes(own, hi, plane)
    mover.step()
    (cotangent,) = tie((out_cotangent,), (x12, mover.right, mover.left))
    cotangent = lax.all_gather(cotangent, "tp", axis=1, tiled=True)
    cotangent = lax.all_gather(cotangent, "lo", axis=0, tiled=True)

    sm12, mixed, xt12, ending, mover.result = call(
        functools.partial(smooth_kernel, rows, tok),
        "smooth",
        lo,
        (x12, x12, taps, decay),
        [
            pl.BlockSpec((1, 2 * tok, wide), lambda n: (n, 0, 0)),
            rim_spec,
            taps_spec,
            mode_spec,
        ],
        [
            shape((2, tokens, LANES), f32),
            shape((tokens, LANES), f32),
            shape((2, tokens, LANES), f32),
            shape((modes, rows, LANES), f32),
            shape((hi * own.shape[0], wide), own.dtype),
        ],
        [up_two, up_one, up_two, mode_spec, held_spec],
        [padded(2), states],
        0,
    )
    mover.step()

    def from_plane(a, distance):
        pairs = [(z + distance, z) for z in range(max(0, -distance), hi - max(0, distance))]
        return lax.ppermute(a, "hi", pairs)

    before = jnp.zeros_like(ending)
    for k in reversed(range(1, hi)):
        before = from_plane(ending, -k) + plane_decay * before
    mover.right, mover.left = tie((mover.right, mover.left), (before,))
    sm0, xt0, field, gated = call(
        functools.partial(field_kernel, rows, tok),
        "field",
        lo,
        (x0, x12, taps, mixed, before, decay, residue, direct),
        [
            pl.BlockSpec((1, 1, tok, wide), lambda n: (n, 0, 0, 0)),
            rim_spec,
            taps_spec,
            up_one,
            mode_spec,
            mode_spec,
            mode_spec,
            skip_spec,
        ],
        [
            shape((tokens, LANES), f32),
            shape((tokens, LANES), f32),
            shape((tokens, LANES), f32),
            shape((length, wide), jnp.bfloat16),
        ],
        [up_one, up_one, up_one, up_wide],
        [padded(1), staged, states],
        0,
    )
    mover.place()
    while mover.done < hi - 1:
        mover.step()

    partial_grad = lax.dot_general(
        cotangent, gated, (((0,), (0,)), ((), ())), preferred_element_type=f32
    ).astype(jnp.bfloat16)
    sums = Sums(partial_grad, hi, plane)
    sums.step()
    mover.right, mover.left = tie((mover.right, mover.left), (sums.to_right, sums.to_left))
    mover.place()
    weights = mover.result

    upstream = jnp.dot(cotangent, weights, preferred_element_type=f32)
    partial_out = project(gated, weights)
    edge = EDGE * rows
    held = modes * rows + 4 * edge
    grad_field, grad_zero, ahead, back_end, grad_skip = call(
        functools.partial(cotangent_kernel, rows, tok),
        "cotangent",
        lo,
        (upstream, sm0, mixed, field, decay, sm12, partial_out),
        [
            down_wide,
            down_one,
            down_one,
            down_one,
            mode_spec,
            whole((2, edge, LANES)),
            held_spec,
        ],
        [
            shape((tokens, LANES), f32),
            shape((tokens, LANES), f32),
            shape((held, LANES), f32),
            shape((modes, rows, LANES), f32),
            shape((rows, LANES), f32),
        ],
        [down_one, down_one, whole((held, LANES)), mode_spec, skip_spec],
        [staged, states, pltpu.VMEM((rows, LANES), f32)],
        0,
    )

    (partial_out,) = tie((partial_out,), (back_end,))
    output = lax.psum_scatter(partial_out, "lo", scatter_dimension=0, tiled=True)
    output = lax.psum_scatter(output, "tp", scatter_dimension=1, tiled=True)
    ahead, back_end = tie((ahead, back_end), (sums.right, sums.left))
    ahead = from_plane(ahead, 1)
    beyond = jnp.zeros_like(back_end)
    for k in reversed(range(2, hi)):
        beyond = from_plane(back_end, k) + plane_decay * beyond
    after = ahead[: modes * rows].reshape(back_end.shape) + beyond * jnp.exp(
        -rate * (length - EDGE)
    )
    ahead = ahead[modes * rows :]

    sums.right, sums.left = tie((sums.right, sums.left), (after, ahead))
    sums.step()
    grads, grad_taps = call(
        functools.partial(back_kernel, rows, tok),
        "back",
        lo,
        (grad_field, grad_zero, sm12, xt0, xt12, after, ahead, decay, residue, direct, taps),
        [
            down_one,
            down_one,
            down_two,
            down_one,
            down_two,
            mode_spec,
            whole((4 * edge, LANES)),
            mode_spec,
            mode_spec,
            skip_spec,
            taps_spec,
        ],
        [
            shape((lo, 3, tok, wide), jnp.bfloat16),
            shape((3, lags, rows, LANES), f32),
        ],
        [grads_spec(3), taps_spec],
        [padded(3), staged, states, pltpu.VMEM((3, lags, rows, LANES), f32)],
        0,
    )
    grads = lax.all_to_all(grads, "lo", 0, 0, tiled=True)
    sums.right, sums.left = tie((sums.right, sums.left), (grad_taps,), 30 * 10**9)
    grad_taps = jnp.sum(grad_taps.reshape(3 * lags * near, members), axis=1)
    part = jnp.concatenate([grad_skip.reshape(-1), grad_taps])
    part = jnp.pad(part, (0, -part.size % wide)).reshape(-1, wide)
    part = jnp.pad(part, ((0, -part.shape[0] % EDGE), (0, 0)))
    small = part
    for k in range(1, hi):
        small = small + lax.ppermute(part, "hi", [(z, (z + k) % hi) for z in range(hi)])
    while sums.done < hi - 1:
        sums.step()

    reduced = sums.finish().astype(jnp.bfloat16).reshape(lo, -1, wide)
    count = reduced.shape[1]
    coarse = small.astype(jnp.bfloat16)
    fine = (small - coarse.astype(f32)).astype(jnp.bfloat16)
    extra = jnp.concatenate([coarse, fine])
    extra = jnp.broadcast_to(extra, (lo,) + extra.shape)
    reduced = jnp.concatenate([reduced, extra], axis=1)[:, None]
    (reduced,) = tie((reduced,), (output,), 30 * 10**9)
    reduced = lax.all_to_all(reduced, "lo", 0, 0, tiled=True)
    grad_weight = join_channels((reduced,), f32, count)[0]
    grad_streams = join_channels((grads,), grads.dtype, tok)
    small = reduced[:, 0, count:].astype(f32)
    small = (small[:, : part.shape[0]] + small[:, part.shape[0] :]).reshape(lo, -1)
    grad_skip = small[:, :wide].reshape(channels)
    grad_short = small[:, wide : wide + 3 * lags * near].reshape(lo, 3, lags, near)
    grad_short = jnp.moveaxis(grad_short, 0, 2)
    return output, grad_streams, grad_short.reshape(3, lags, groups), grad_skip, grad_weight


def solution(mesh):
    count, parts = mesh.shape["ctx"], mesh.shape["tp"]
    lo = math.gcd(count, 8)
    cut = Mesh(mesh.devices.reshape(count // lo, lo, parts), ("hi", "lo", "tp"))
    ctx = ("hi", "lo")
    return jax.shard_map(
        shards,
        mesh=cut,
        in_specs=(
            P(None, ctx, "tp"),
            P(None, None, "tp"),
            P(None, "tp"),
            P(None, "tp"),
            P("tp"),
            P(ctx, "tp"),
            P(ctx, "tp"),
        ),
        out_specs=(
            P(ctx, "tp"),
            P(None, ctx, "tp"),
            P(None, None, "tp"),
            P("tp"),
            P(ctx, "tp"),
        ),
        check_vma=False,
    )
```
